32 devices in a mesh: px: 4 (over z), py: 4 (over y, core), lev: 2 (over x).
Axes of the slice: x: 2, y: 2, z: 4, core: 2. Of those that a mesh axis runs over, the one named last changes fastest.
Arguments:
- pressure: float32 [8, 512, 512], P('lev', 'px', 'py'), may hold values from -6 to 6
- wind_east: float32 [8, 512, 512], P('lev', 'px', 'py'), may hold values from -6 to 6
- wind_north: float32 [8, 512, 512], P('lev', 'px', 'py'), may hold values from -6 to 6
- wind_up: float32 [8, 512, 512], P('lev', 'px', 'py'), may hold values from -6 to 6
- stiffness: float32 [8, 512, 512], P('lev', 'px', 'py'), may hold values from 0.3 to 1
- edge_table: int32 [4, 4, 4], replicated, may hold values from 0 to 7
- remap_source: int32 [65536], P(('px', 'py')), may hold values from 0 to 16383
- remap_weight: float32 [65536], P(('px', 'py')), may hold values from 0.25 to 1
- remap_owner: int32 [65536, 1], P(('px', 'py')), may hold values from 0 to 3; in each aligned block of 4096 rows (0 to 4095, 4096 to 8191, ...) at most 2048 rows name the same one
- latlon_cell: int32 [131072], P(('px', 'py')), may hold values from 0 to 2047
Outputs:
- final_pressure: float32 [8, 512, 512], P('lev', 'px', 'py')
- latlon_fields: float32 [4, 8, 32768], P(None, 'lev', ('px', 'py'))
The draws below stay inside these ranges and needn't reach their ends.
Inputs may be any that keep to these rules, and one draw needn't show every extreme that they name: `remap_owner`: among the 4096 entries of one tile no owner is named more than 2048 times, and in every draw some tile names some owner exactly 2048 times.
All inputs are finite; a program needn't handle non-finite values.
Results may differ from the reference program's by a relative error of at most 0.0003.
Values sent between devices are 32-bit elements; how exact they have to be, the bound alone decides.
A program may use at most 64 MiB of HBM per device.

```python
import math
import jax
import jax.numpy as jnp
import numpy as np
from jax import lax

TILE = 128
SUBSTEPS = 4
LV = 8
NX = 512
NY = 512
TILES = 16
ENTRIES = 4096
CELLS = 2048
SLOTS = 2048
N_PX = 4
N_PY = 4


def place_ends(drawn, stream_key, low, top_value):
    place = [jax.random.randint(jax.random.fold_in(stream_key, axis), (), 0, length) for axis, length in enumerate(drawn.shape)]
    main_axis = drawn.shape.index(max(drawn.shape))
    beside = place[:main_axis] + [(place[main_axis] + 1) % drawn.shape[main_axis]] + place[main_axis + 1:]
    return drawn.at[tuple(place)].set(low).at[tuple(beside)].set(top_value)


def steps_of(own_key, shape, pieces, low, largest):
    level, own = 1.0, jax.random.fold_in(own_key, 6)
    for axis_at, shards_of in pieces:
        heights = jnp.exp(jax.random.uniform(jax.random.fold_in(own, axis_at), (shards_of,), jnp.float32, low / len(pieces), largest / len(pieces)))
        level = level * jnp.repeat(heights, shape[axis_at] // shards_of).reshape([-1 if axis == axis_at else 1 for axis in range(len(shape))])
    return level


def shared_out(rng, own, number, rows, count, top, reach, slope):
    order = jax.random.permutation(rng, count)
    heavy_load, usual = shares(count, rows * top, reach, slope, True), shares(count, rows * top, reach, slope, False)
    places = jnp.arange(count)

    def named(sizes, offset_by):
        used = int((sizes > 0).sum())
        fixed = max(1, used // 4)
        shifted = fixed + (places - fixed + offset_by * (used - fixed)) % max(1, count - fixed)
        return jnp.zeros((count,), jnp.int32).at[order[jnp.where(places < fixed, places, shifted)]].set(jnp.asarray(sizes, jnp.int32))

    sizes = jnp.where(number % 4 == 0, named(heavy_load, number // 4), named(usual, number - number // 4 - 1))
    mixed = jax.random.permutation(jax.random.fold_in(own, 3), count)
    donor, taker = mixed[0:count // 2 * 2:2], mixed[1:count // 2 * 2:2]
    room = jnp.minimum(sizes[donor] - 1, reach - sizes[taker]) // 2
    room = jnp.where((donor == order[0]) | (taker == order[0]) | (sizes[taker] == 0), 0, jnp.maximum(room, 0))
    shifted = jax.random.randint(jax.random.fold_in(own, 4), (count // 2,), 0, 1 << 20) % (room + 1)
    sizes = sizes.at[donor].add(-shifted).at[taker].add(shifted)
    labels = jnp.searchsorted(jnp.cumsum(sizes), jnp.arange(rows * top), side="right").astype(jnp.int32)
    grid = labels.reshape(top, rows).T
    grid = grid[jax.random.permutation(jax.random.fold_in(own, 1), rows)]
    offset_by = jax.random.randint(jax.random.fold_in(own, 2), (rows, 1), 0, top)
    return jnp.take_along_axis(grid, (jnp.arange(top)[None, :] + offset_by) % top, axis=1)


def shares(count, total, limit, skew, full):
    weights = [(1 << 20) // math.isqrt(standing ** skew) + 1 for standing in range(1, count + 1)]
    largest = limit if full else min(limit, max(-(-total // count), total * weights[0] // sum(weights)))
    least = 1 if total - largest >= count - 1 else 0
    given, surplus = [largest] + [least] * (count - 1), total - largest - least * (count - 1)
    while surplus > 0:
        candidates = [i for i in range(1, count) if given[i] < largest] or [i for i in range(1, count) if given[i] < limit]
        pool, left = sum([weights[i] for i in candidates]), surplus
        for i in candidates:
            addition = min(limit - given[i], max(1, left * weights[i] // pool), surplus)
            given[i] = given[i] + addition
            surplus = surplus - addition
    return np.array(given)


def gaussian(key, shape, spread, bound, pieces=(), kind=jnp.bfloat16):
    drawn = jax.random.normal(key, shape, jnp.float32) * spread
    if len(pieces) > 0:
        drawn = steps_of(key, shape, pieces, -0.22, 0.18) * drawn
    return jnp.clip(drawn, min=-bound, max=bound).astype(kind)


def setup_inputs(seed: int = 0) -> dict:
    key_list = jax.random.split(jax.random.key(seed), 11)
    pressure = gaussian(key_list[0], (LV, NX, NY), 1.0, 6.0, ((0, 2), (1, 4), (2, 4)), jnp.float32)
    wind_east = gaussian(key_list[1], (LV, NX, NY), 1.0, 6.0, ((0, 2), (1, 4), (2, 4)), jnp.float32)
    wind_north = gaussian(key_list[2], (LV, NX, NY), 1.0, 6.0, ((0, 2), (1, 4), (2, 4)), jnp.float32)
    wind_up = gaussian(key_list[3], (LV, NX, NY), 1.0, 6.0, ((0, 2), (1, 4), (2, 4)), jnp.float32)
    stiffness = jnp.clip(jnp.exp(math.log(1.0) - 1.2039728 * jax.random.uniform(key_list[4], (LV, NX, NY), jnp.float32) ** steps_of(key_list[4], (LV, NX, NY), ((0, 2), (1, 4), (2, 4)), -0.2, 0.2)), 0.3, 1.0)
    edge_table = place_ends(jax.random.randint(key_list[5], (NX // TILE, NY // TILE, 4), 0, 8), jax.random.fold_in(key_list[5], 1), 0, 7).astype(jnp.int32)
    remap_source = place_ends(jax.random.randint(key_list[6], (TILES * ENTRIES,), 0, TILE * TILE), jax.random.fold_in(key_list[6], 1), 0, (TILE * TILE) - 1).astype(jnp.int32)
    remap_weight = jnp.clip(0.25 + 0.75 * jax.random.uniform(key_list[7], (TILES * ENTRIES,), jnp.float32) ** steps_of(key_list[7], (TILES * ENTRIES,), ((0, 16),), -0.2, 0.2), 0.25, 1.0)
    remap_owner_keys = jax.random.split(jax.random.fold_in(key_list[8], 1), (TILES * ENTRIES) // ENTRIES)
    remap_owner_turns = jax.random.permutation(jax.random.fold_in(key_list[8], 3), (TILES * ENTRIES) // ENTRIES)
    remap_owner = jax.vmap(lambda own, number: shared_out(jax.random.fold_in(key_list[8], 2), own, number, ENTRIES, N_PX, 1, SLOTS, 2))(remap_owner_keys, remap_owner_turns).reshape((TILES * ENTRIES, 1))
    latlon_cell = place_ends(jax.random.randint(key_list[9], (TILES * N_PX * SLOTS,), 0, CELLS), jax.random.fold_in(key_list[9], 1), 0, CELLS - 1).astype(jnp.int32)
    return dict(pressure=pressure, wind_east=wind_east, wind_north=wind_north, wind_up=wind_up, stiffness=stiffness, edge_table=edge_table, remap_source=remap_source, remap_weight=remap_weight, remap_owner=remap_owner, latlon_cell=latlon_cell)


horiz_coef = 0.45
vert_coef = 0.3
roll_plan = ((1, 2), (1, 3), (-1, 2), (-1, 3))


def rim_stack(field):
    blocks = field.reshape(LV, N_PX, TILE, N_PY, TILE)
    west_rim = blocks[:, :, 0, :, :]
    east_rim = blocks[:, :, -1, :, :]
    south_rim = jnp.transpose(blocks[:, :, :, :, 0], (0, 1, 3, 2))
    north_rim = jnp.transpose(blocks[:, :, :, :, -1], (0, 1, 3, 2))
    return jnp.stack([west_rim, south_rim, east_rim, north_rim])


def turn_pair(first, second, quarter_turns):
    new_first = jnp.where(quarter_turns == 0, first, jnp.where(quarter_turns == 1, -second, jnp.where(quarter_turns == 2, -first, second)))
    new_second = jnp.where(quarter_turns == 0, second, jnp.where(quarter_turns == 1, first, jnp.where(quarter_turns == 2, -second, -first)))
    return new_first, new_second


def ghost_sets(fields, edge_table, vector):
    stacks = [rim_stack(field) for field in fields]
    result = []
    for facing in range(4):
        amount, axis_num = roll_plan[facing]
        edge_code = edge_table[:, :, facing]
        quarter_turns = edge_code % 4
        flipped = edge_code // 4
        wanted = (facing + 2 + quarter_turns) % 4
        picked = []
        for stacked in stacks:
            rolled = jnp.roll(stacked, amount, axis=axis_num)
            chosen = rolled[0]
            for option in range(1, 4):
                chosen = jnp.where(wanted[None, :, :, None] == option, rolled[option], chosen)
            chosen = jnp.where(flipped[None, :, :, None] == 1, chosen[..., ::-1], chosen)
            picked.append(chosen)
        if vector:
            picked = list(turn_pair(picked[0], picked[1], quarter_turns[None, :, :, None]))
        result.append(picked)
    return result


def spreads(field, ghosts):
    west_ghost, south_ghost, east_ghost, north_ghost = ghosts
    blocks = field.reshape(LV, N_PX, TILE, N_PY, TILE)
    east_val = jnp.concatenate([blocks[:, :, 1:], east_ghost[:, :, None]], axis=2)
    west_val = jnp.concatenate([west_ghost[:, :, None], blocks[:, :, :-1]], axis=2)
    north_val = jnp.concatenate([blocks[..., 1:], jnp.transpose(north_ghost, (0, 1, 3, 2))[..., None]], axis=4)
    south_val = jnp.concatenate([jnp.transpose(south_ghost, (0, 1, 3, 2))[..., None], blocks[..., :-1]], axis=4)
    return (east_val - west_val).reshape(LV, NX, NY), (north_val - south_val).reshape(LV, NX, NY)


def ranking(owner_row):
    onehot = (owner_row[:, None] == jnp.arange(N_PX, dtype=jnp.int32)[None, :]).astype(jnp.int32)
    counts = jnp.cumsum(onehot, axis=0)
    return jnp.sum(counts * onehot, axis=1) - 1


def pick_columns(column_block, sources):
    return column_block[:, :, sources]


def reference(pressure, wind_east, wind_north, wind_up, stiffness, edge_table, remap_source, remap_weight, remap_owner, latlon_cell):
    level_pos = lax.broadcasted_iota(jnp.int32, pressure.shape, 0)
    summit_mask = level_pos == LV - 1
    zero_layer = jnp.zeros((1, NX, NY), jnp.float32)
    for substep in range(SUBSTEPS):
        press_ghosts = ghost_sets([pressure], edge_table, False)
        east_diff, north_diff = spreads(pressure, [ghost[0] for ghost in press_ghosts])
        wind_east = wind_east - horiz_coef * east_diff
        wind_north = wind_north - horiz_coef * north_diff
        press_up = jnp.concatenate([pressure[1:], zero_layer], axis=0)
        wind_up = jnp.where(summit_mask, 0.0, wind_up - vert_coef * (press_up - pressure))
        wind_low = jnp.concatenate([zero_layer, wind_up[:-1]], axis=0)
        wind_ghosts = ghost_sets([wind_east, wind_north], edge_table, True)
        east_flow = spreads(wind_east, [ghost[0] for ghost in wind_ghosts])[0]
        north_flow = spreads(wind_north, [ghost[1] for ghost in wind_ghosts])[1]
        pressure = pressure - stiffness * (horiz_coef * (east_flow + north_flow) + vert_coef * (wind_up - wind_low))
    fields = jnp.stack([pressure, wind_east, wind_north, wind_up])
    columns = fields.reshape(4, LV, N_PX, TILE, N_PY, TILE).transpose(2, 4, 0, 1, 3, 5).reshape(TILES, 4, LV, TILE * TILE)
    sources = remap_source.reshape(TILES, ENTRIES)
    weights = remap_weight.reshape(TILES, ENTRIES)
    owners = remap_owner[:, 0].reshape(TILES, ENTRIES)
    payload = jax.vmap(pick_columns)(columns, sources) * weights[:, None, None, :]
    slot_rank = lax.map(ranking, owners)
    tile_index = jnp.arange(TILES, dtype=jnp.int32)[:, None]
    tile_first = tile_index // N_PY
    tile_second = tile_index % N_PY
    cell_table = latlon_cell.reshape(N_PX, N_PY, N_PX, SLOTS)
    target_cell = cell_table[owners, tile_second, tile_first, slot_rank]
    destination = (owners * N_PY + tile_second) * CELLS + target_cell
    flat_values = payload.transpose(1, 2, 0, 3).reshape(4, LV, TILES * ENTRIES)
    latlon_fields = jnp.zeros((4, LV, TILES * CELLS), jnp.float32).at[:, :, destination.reshape(-1)].add(flat_values)
    return pressure, latlon_fields
```

```python
import functools

import jax
import jax.numpy as jnp
from jax import lax
from jax.experimental import pallas as pl
from jax.experimental.pallas import tpu as pltpu
from jax.sharding import PartitionSpec as P

SUBSTEPS = 4
A = 0.45
B = 0.3
LANES = 128
BLOCK = 256
MESH = pl.DeviceIdType.MESH


def iota(shape, dim):
    return lax.broadcasted_iota(jnp.int32, shape, dim)


def parts2(x):
    high = x.astype(jnp.bfloat16)
    return high, (x - high.astype(jnp.float32)).astype(jnp.bfloat16)


def dot_nt(a, b):
    return lax.dot_general(a, b, (((1,), (1,)), ((), ())), preferred_element_type=jnp.float32)


def substeps_kernel(
    sizes,
    edges,
    p_in,
    we_in,
    wn_in,
    wu_in,
    st,
    p,
    we,
    wn,
    wu,
    psend,
    precv,
    wsend,
    wrecv,
    above,
    below,
    wu_below,
    flipped_cols,
    ghost_rows,
    pre,
    st_rims,
    psend_sem,
    precv_sem,
    wsend_sem,
    wrecv_sem,
    up_sems,
    down_sems,
    wub_sems,
):
    n_px, n_py, n_lev = sizes
    levels, tile, _ = p_in.shape
    last = tile - 1
    ix, iy, iz = lax.axis_index("px"), lax.axis_index("py"), lax.axis_index("lev")
    targets = (
        {"px": lax.rem(ix + 1, n_px)},
        {"py": lax.rem(iy + 1, n_py)},
        {"px": lax.rem(ix + n_px - 1, n_px)},
        {"py": lax.rem(iy + n_py - 1, n_py)},
    )
    has_above, has_below = iz < n_lev - 1, iz > 0

    barrier = pltpu.get_barrier_semaphore()
    for target in targets:
        pl.semaphore_signal(barrier, inc=1, device_id=target, device_id_type=MESH)

    @pl.when(has_above)
    def _():
        pl.semaphore_signal(barrier, inc=1, device_id={"lev": iz + 1}, device_id_type=MESH)

    @pl.when(has_below)
    def _():
        pl.semaphore_signal(barrier, inc=1, device_id={"lev": iz - 1}, device_id_type=MESH)

    def rim_copy(send, recv, send_sem, recv_sem, t, s):
        return pltpu.make_async_remote_copy(
            src_ref=send.at[t],
            dst_ref=recv.at[t, s],
            send_sem=send_sem.at[t, s],
            recv_sem=recv_sem.at[t, s],
            device_id=targets[s],
            device_id_type=MESH,
        )

    p_copy = functools.partial(rim_copy, psend, precv, psend_sem, precv_sem)
    w_copy = functools.partial(rim_copy, wsend, wrecv, wsend_sem, wrecv_sem)

    def up_copy(t):
        return pltpu.make_async_remote_copy(
            src_ref=p.at[levels - 1],
            dst_ref=below.at[t],
            send_sem=up_sems.at[0, t],
            recv_sem=up_sems.at[1, t],
            device_id={"lev": iz + 1},
            device_id_type=MESH,
        )

    def down_copy(t):
        return pltpu.make_async_remote_copy(
            src_ref=p.at[0],
            dst_ref=above.at[t],
            send_sem=down_sems.at[0, t],
            recv_sem=down_sems.at[1, t],
            device_id={"lev": iz - 1},
            device_id_type=MESH,
        )

    def wub_copy():
        return pltpu.make_async_remote_copy(
            src_ref=wu_in.at[levels - 1],
            dst_ref=wu_below,
            send_sem=wub_sems.at[0],
            recv_sem=wub_sems.at[1],
            device_id={"lev": iz + 1},
            device_id_type=MESH,
        )

    row, lane = iota((tile, tile), 0), iota((tile, tile), 1)
    edge_lanes = (lane == 0) | (lane == last)
    rim_lane = iota((levels, tile), 1)
    first_lane, last_lane = rim_lane == 0, rim_lane == last

    def d_rows(f):
        return jnp.where(row == last, 0.0, pltpu.roll(f, last, 0)) - jnp.where(
            row == 0, 0.0, pltpu.roll(f, 1, 0)
        )

    def d_lanes(f):
        return jnp.where(lane == last, 0.0, pltpu.roll(f, last, 1)) - jnp.where(
            lane == 0, 0.0, pltpu.roll(f, 1, 1)
        )

    def columns(fields):
        packed = jnp.zeros((tile, tile), jnp.float32)
        for j, f in enumerate(fields):
            packed = jnp.where((lane >> 1) == j, pltpu.roll(f, 2 * j + 1, 1), packed)
        flipped_cols[...] = packed.T
        count = len(fields)
        return (
            flipped_cols[pl.ds(1, count, stride=2), :],
            flipped_cols[pl.ds(0, count, stride=2), :],
        )

    def lane_terms(south, north):
        ghost_rows[pl.ds(0, levels, stride=2), :] = north
        ghost_rows[pl.ds(1, levels, stride=2), :] = south
        turned = ghost_rows[...].T
        return [
            jnp.where(edge_lanes, pltpu.roll(turned, (tile - 2 * j - 1) % tile, 1), 0.0)
            for j in range(levels)
        ]

    codes = [edges[ix, iy, s] for s in range(4)]
    turns = [c & 3 for c in codes]
    wanted = [(s + 2 + turns[s]) & 3 for s in range(4)]
    place = iota((2 * levels, tile), 1)
    order = [jnp.where((codes[s] >> 2) == 1, last - place, place) for s in range(4)]
    low = iota((2 * levels, tile), 0) < levels

    def picked_rim(recv, t, s):
        rim = recv[t, s, 0]
        for k in range(1, 4):
            rim = jnp.where(wanted[s] == k, recv[t, s, k], rim)
        return rim

    def pressure_ghosts(t):
        ghosts = []
        for s in (0, 2):
            for k in (s, s + 1):
                p_copy(t, k).wait_recv()
            both = jnp.concatenate([picked_rim(precv, t, s), picked_rim(precv, t, s + 1)], axis=0)
            both = jnp.take_along_axis(both, jnp.where(low, order[s], order[s + 1]), axis=1)
            ghosts += [both[:levels], both[levels:]]
        return ghosts

    def wind_ghosts(t):
        ghosts = []
        for s in range(4):
            w_copy(t, s).wait_recv()
            both = jnp.take_along_axis(picked_rim(wrecv, t, s), order[s], axis=1)
            a, b = both[:levels], both[levels:]
            r = turns[s]
            if s % 2 == 0:
                ghost = jnp.where(r == 0, a, jnp.where(r == 1, -b, jnp.where(r == 2, -a, b)))
            else:
                ghost = jnp.where(r == 0, b, jnp.where(r == 1, a, jnp.where(r == 2, -b, -a)))
            ghosts.append(ghost)
        return ghosts

    def corner(first, second, end):
        if end == 0:
            return jnp.where(first_lane, first, 0.0) - jnp.where(last_lane, pltpu.roll(second, last, 1), 0.0)
        return jnp.where(first_lane, pltpu.roll(first, 1, 1), 0.0) - jnp.where(last_lane, second, 0.0)

    p[...] = p_in[...]
    south, north = columns([p_in[j] for j in range(levels)])
    psend[0, 0] = p_in[:, 0, :]
    psend[0, 1] = south
    psend[0, 2] = p_in[:, last, :]
    psend[0, 3] = north

    pl.semaphore_wait(barrier, 4 + has_above.astype(jnp.int32) + has_below.astype(jnp.int32))
    for s in range(4):
        p_copy(0, s).start()

    @pl.when(has_above)
    def _():
        wub_copy().start()

    @pl.when(jnp.logical_not(has_below))
    def _():
        wu_below[...] = jnp.zeros((tile, tile), jnp.float32)

    ghost_rows[...] = jnp.zeros((tile, tile), jnp.float32)
    south, north = columns([st[j] for j in range(levels)])
    st_rims[0] = st[:, 0, :] * A
    st_rims[1] = south * A
    st_rims[2] = st[:, last, :] * A
    st_rims[3] = north * A
    we[...] = we_in[...]
    wn[...] = wn_in[...]
    wu[...] = wu_in[...]

    def substep(t, carry):
        @pl.when(has_above)
        def _():
            up_copy(t).start()

        @pl.when(has_below)
        def _():
            down_copy(t).start()

        for j in range(levels):
            we[j] = we[j] - A * d_rows(p[j])
            wn[j] = wn[j] - A * d_lanes(p[j])
        south, north = columns([we[j] for j in range(levels)] + [wn[j] for j in range(levels)])
        pre[0, :levels] = we[:, 0, :]
        pre[0, levels:] = wn[:, 0, :]
        pre[1] = south
        pre[2, :levels] = we[:, last, :]
        pre[2, levels:] = wn[:, last, :]
        pre[3] = north
        for j in range(levels - 1):
            wu[j] = wu[j] - B * (p[j + 1] - p[j])

        gw, gs, ge, gn = [A * g for g in pressure_ghosts(t)]
        wsend[t, 0, :levels] = pre[0, :levels] + gw
        wsend[t, 0, levels:] = pre[0, levels:] + corner(gs, gn, 0)
        wsend[t, 1, :levels] = pre[1, :levels] + corner(gw, ge, 0)
        wsend[t, 1, levels:] = pre[1, levels:] + gs
        wsend[t, 2, :levels] = pre[2, :levels] - ge
        wsend[t, 2, levels:] = pre[2, levels:] + corner(gs, gn, last)
        wsend[t, 3, :levels] = pre[3, :levels] + corner(gw, ge, last)
        wsend[t, 3, levels:] = pre[3, levels:] - gn
        for s in range(4):
            w_copy(t, s).start()

        we[:, 0, :] = we[:, 0, :] + gw
        we[:, last, :] = we[:, last, :] - ge
        terms = lane_terms(gs, -gn)
        for j in range(levels):
            wn[j] = wn[j] + terms[j]

        @pl.when(has_above)
        def _():
            up_copy(t).wait_send()
            down_copy(t).wait_recv()
            wu[levels - 1] = wu[levels - 1] - B * (above[t] - p[levels - 1])

        @pl.when(jnp.logical_not(has_above))
        def _():
            wu[levels - 1] = jnp.zeros((tile, tile), jnp.float32)

        @pl.when(has_below & (t == 0))
        def _():
            wub_copy().wait_recv()

        @pl.when(has_below)
        def _():
            down_copy(t).wait_send()
            up_copy(t).wait_recv()
            wu_below[...] = wu_below[...] - B * (p[0] - below[t])

        for j in range(levels):
            under = wu_below[...] if j == 0 else wu[j - 1]
            p[j] = p[j] - st[j] * (A * (d_rows(we[j]) + d_lanes(wn[j])) + B * (wu[j] - under))
        south, north = columns([p[j] for j in range(levels)])
        pre[0, :levels] = p[:, 0, :]
        pre[1, :levels] = south
        pre[2, :levels] = p[:, last, :]
        pre[3, :levels] = north

        gw, gs, ge, gn = wind_ghosts(t)

        @pl.when(t < SUBSTEPS - 1)
        def _():
            psend[t + 1, 0] = pre[0, :levels] + st_rims[0] * (gw + corner(gs, gn, 0))
            psend[t + 1, 1] = pre[1, :levels] + st_rims[1] * (gs + corner(gw, ge, 0))
            psend[t + 1, 2] = pre[2, :levels] + st_rims[2] * (corner(gs, gn, last) - ge)
            psend[t + 1, 3] = pre[3, :levels] + st_rims[3] * (corner(gw, ge, last) - gn)
            for s in range(4):
                p_copy(t + 1, s).start()

        p[:, 0, :] = p[:, 0, :] + st_rims[0] * gw
        p[:, last, :] = p[:, last, :] - st_rims[2] * ge
        terms = lane_terms(st_rims[1] * gs, -(st_rims[3] * gn))
        for j in range(levels):
            p[j] = p[j] + terms[j]
        return carry

    lax.fori_loop(0, SUBSTEPS, substep, 0)

    def drain(t, carry):
        for s in range(4):
            p_copy(t, s).wait_send()
            w_copy(t, s).wait_send()
        return carry

    lax.fori_loop(0, SUBSTEPS, drain, 0)

    @pl.when(has_above)
    def _():
        wub_copy().wait_send()


def run_substeps(sizes, pressure, wind_east, wind_north, wind_up, stiffness, edge_table):
    levels, tile, _ = pressure.shape
    field = jax.ShapeDtypeStruct(pressure.shape, jnp.float32)
    in_vmem = pl.BlockSpec(memory_space=pltpu.VMEM)
    n = SUBSTEPS
    return pl.pallas_call(
        functools.partial(substeps_kernel, sizes),
        out_shape=[field] * 4,
        in_specs=[pl.BlockSpec(memory_space=pltpu.SMEM)] + [in_vmem] * 5,
        out_specs=[in_vmem] * 4,
        scratch_shapes=[
            pltpu.VMEM((n, 4, levels, tile), jnp.float32),
            pltpu.VMEM((n, 4, 4, levels, tile), jnp.float32),
            pltpu.VMEM((n, 4, 2 * levels, tile), jnp.float32),
            pltpu.VMEM((n, 4, 4, 2 * levels, tile), jnp.float32),
            pltpu.VMEM((n, tile, tile), jnp.float32),
            pltpu.VMEM((n, tile, tile), jnp.float32),
            pltpu.VMEM((tile, tile), jnp.float32),
            pltpu.VMEM((tile, tile), jnp.float32),
            pltpu.VMEM((tile, tile), jnp.float32),
            pltpu.VMEM((4, 2 * levels, tile), jnp.float32),
            pltpu.VMEM((4, levels, tile), jnp.float32),
            pltpu.SemaphoreType.DMA((n, 4)),
            pltpu.SemaphoreType.DMA((n, 4)),
            pltpu.SemaphoreType.DMA((n, 4)),
            pltpu.SemaphoreType.DMA((n, 4)),
            pltpu.SemaphoreType.DMA((2, n)),
            pltpu.SemaphoreType.DMA((2, n)),
            pltpu.SemaphoreType.DMA((2,)),
        ],
        compiler_params=pltpu.CompilerParams(
            collective_id=0, has_side_effects=True, vmem_limit_bytes=32 * 2**20
        ),
    )(edge_table, pressure, wind_east, wind_north, wind_up, stiffness)


def slots_kernel(owner_count, slot_count, owner, source, weight, slot_source, slot_weight):
    rows = owner.shape[0]
    slot_rows = slot_source.shape[0]
    names = owner[...]
    up_to = (iota((LANES, LANES), 0) <= iota((LANES, LANES), 1)).astype(jnp.bfloat16)
    ones = jnp.ones((LANES, LANES), jnp.bfloat16)
    before = (iota((rows, rows), 0) > iota((rows, rows), 1)).astype(jnp.bfloat16)

    def count(o, rank):
        named = names == o
        hot = named.astype(jnp.float32).astype(jnp.bfloat16)
        within = jnp.dot(hot, up_to, preferred_element_type=jnp.float32)
        total = jnp.dot(hot, ones, preferred_element_type=jnp.float32).astype(jnp.bfloat16)
        earlier = jnp.dot(before, total, preferred_element_type=jnp.float32)
        return jnp.where(named, within + earlier - 1.0, rank)

    rank = lax.fori_loop(0, owner_count, count, jnp.zeros(names.shape, jnp.float32))
    slot = names * slot_count + rank.astype(jnp.int32)
    slot_high, slot_low = slot >> 7, slot & (LANES - 1)
    src = source[...]
    w = weight[...]
    w1 = w.astype(jnp.bfloat16).astype(jnp.float32)
    w2 = (w - w1).astype(jnp.bfloat16).astype(jnp.float32)
    w3 = w - w1 - w2
    pieces = [(src >> 7).astype(jnp.float32), (src & (LANES - 1)).astype(jnp.float32), w1, w2, w3]
    high_place, low_place = iota((slot_rows, LANES), 0), iota((LANES, LANES), 0)
    total = jnp.zeros((len(pieces) * slot_rows, LANES), jnp.float32)
    for r in range(rows):
        here = high_place == slot_high[r : r + 1]
        left = jnp.concatenate([jnp.where(here, piece[r : r + 1], 0.0) for piece in pieces], axis=0)
        right = jnp.where(low_place == slot_low[r : r + 1], 1.0, 0.0)
        total += dot_nt(left.astype(jnp.bfloat16), right.astype(jnp.bfloat16))
    part = [total[k * slot_rows : (k + 1) * slot_rows] for k in range(len(pieces))]
    slot_source[...] = (part[0] * LANES + part[1]).astype(jnp.int32)
    slot_weight[...] = part[2] + part[3] + part[4]


def take_kernel(p, we, wn, wu, slot_source, slot_weight, payload, high, low):
    levels, tile, _ = p.shape
    half = tile // 2
    for q, field in enumerate((p, we, wn, wu)):
        for l in range(levels):
            h, d = parts2(field[l].T)
            at = pl.ds((q * levels + l) * half, half)
            high[at, :tile], high[at, tile:] = h[:half], h[half:]
            low[at, :tile], low[at, tile:] = d[:half], d[half:]
    count = 4 * levels

    def step(b, carry):
        src = jnp.concatenate([slot_source[pl.ds(2 * b, 1), :], slot_source[pl.ds(2 * b + 1, 1), :]], axis=1)
        w = jnp.concatenate([slot_weight[pl.ds(2 * b, 1), :], slot_weight[pl.ds(2 * b + 1, 1), :]], axis=1)
        x, y = src >> 7, src & (tile - 1)
        line = x + jnp.where(y >= half, tile, 0)
        hot = jnp.where(iota((2 * tile, BLOCK), 0) == line, 1.0, 0.0).astype(jnp.bfloat16)
        picked = jnp.dot(high[...], hot, preferred_element_type=jnp.float32)
        picked += jnp.dot(low[...], hot, preferred_element_type=jnp.float32)
        mask = jnp.where(iota((half, BLOCK), 0) == (y & (half - 1)), w, 0.0)
        payload[:, pl.ds(pl.multiple_of(b * BLOCK, BLOCK), BLOCK)] = jnp.sum(
            picked.reshape(count, half, BLOCK) * mask[None], axis=1
        )
        return carry

    lax.fori_loop(0, payload.shape[1] // BLOCK, step, 0)


def land_kernel(arrived, cell, out, total):
    count = arrived.shape[0]
    groups = out.shape[1] // BLOCK
    total[...] = jnp.zeros(total.shape, jnp.float32)

    def step(b, carry):
        c = jnp.concatenate([cell[pl.ds(2 * b, 1), :], cell[pl.ds(2 * b + 1, 1), :]], axis=1)
        values = arrived[:, pl.ds(pl.multiple_of(b * BLOCK, BLOCK), BLOCK)]
        h = values.astype(jnp.bfloat16).astype(jnp.float32)
        group = c >> 8
        spread = [jnp.where(group == g, h, 0.0) for g in range(groups)]
        spread += [jnp.where(group == g, values - h, 0.0) for g in range(groups)]
        hot = jnp.where(iota((BLOCK, BLOCK), 0) == (c & (BLOCK - 1)), 1.0, 0.0)
        total[...] += dot_nt(jnp.concatenate(spread, axis=0).astype(jnp.bfloat16), hot.astype(jnp.bfloat16))
        return carry

    lax.fori_loop(0, arrived.shape[1] // BLOCK, step, 0)
    for g in range(groups):
        out[:, g * BLOCK : (g + 1) * BLOCK] = (
            total[g * count : (g + 1) * count] + total[(groups + g) * count : (groups + g + 1) * count]
        )


def local_call(kernel, out_shape, scratch=()):
    return pl.pallas_call(
        kernel,
        out_shape=out_shape,
        scratch_shapes=list(scratch),
        compiler_params=pltpu.CompilerParams(vmem_limit_bytes=40 * 2**20),
    )


def per_device(
    sizes,
    pressure,
    wind_east,
    wind_north,
    wind_up,
    stiffness,
    edge_table,
    remap_source,
    remap_weight,
    remap_owner,
    latlon_cell,
):
    levels, tile, _ = pressure.shape
    owner_count = sizes[0]
    slots = latlon_cell.shape[0]
    slot_count = slots // owner_count
    cell_count = tile * tile // 8
    count = 4 * levels
    f32 = jnp.float32
    slot_source, slot_weight = local_call(
        functools.partial(slots_kernel, owner_count, slot_count),
        [
            jax.ShapeDtypeStruct((slots // LANES, LANES), jnp.int32),
            jax.ShapeDtypeStruct((slots // LANES, LANES), f32),
        ],
    )(
        remap_owner.reshape(-1, LANES),
        remap_source.reshape(-1, LANES),
        remap_weight.reshape(-1, LANES),
    )
    fields = run_substeps(sizes, pressure, wind_east, wind_north, wind_up, stiffness, edge_table)
    payload = local_call(
        take_kernel,
        jax.ShapeDtypeStruct((count, slots), f32),
        [pltpu.VMEM((count * tile // 2, 2 * tile), jnp.bfloat16)] * 2,
    )(*fields, slot_source, slot_weight)
    arrived = lax.all_to_all(payload, "px", split_axis=1, concat_axis=1, tiled=True)
    groups = cell_count // BLOCK
    latlon = local_call(
        land_kernel,
        jax.ShapeDtypeStruct((count, cell_count), f32),
        [pltpu.VMEM((2 * groups * count, BLOCK), f32)],
    )(arrived, latlon_cell.reshape(-1, LANES))
    return fields[0], latlon.reshape(4, levels, cell_count)


def solution(mesh):
    field = P("lev", "px", "py")
    entries = P(("px", "py"))
    sizes = (mesh.shape["px"], mesh.shape["py"], mesh.shape["lev"])
    return jax.shard_map(
        functools.partial(per_device, sizes),
        mesh=mesh,
        in_specs=(field,) * 5 + (P(), entries, entries, P(("px", "py"), None), entries),
        out_specs=(field, P(None, "lev", ("px", "py"))),
        check_vma=False,
    )
```

```python
import functools

import jax
import jax.numpy as jnp
from jax import lax
from jax.experimental import pallas as pl
from jax.experimental.pallas import tpu as pltpu
from jax.sharding import PartitionSpec as P

SUBSTEPS = 4
A = 0.45
B = 0.3
LANES = 128
BLOCK = 256
MESH = pl.DeviceIdType.MESH


def iota(shape, dim):
    return lax.broadcasted_iota(jnp.int32, shape, dim)


def parts2(x):
    high = x.astype(jnp.bfloat16)
    return high, (x - high.astype(jnp.float32)).astype(jnp.bfloat16)


def dot_nt(a, b):
    return lax.dot_general(a, b, (((1,), (1,)), ((), ())), preferred_element_type=jnp.float32)


def whole_kernel(
    sizes,
    edges,
    p_in,
    we_in,
    wn_in,
    wu_in,
    st_in,
    owner_in,
    source_in,
    weight_in,
    cell_in,
    p,
    latlon,
    we,
    wn,
    wu,
    st,
    owner,
    source,
    weight,
    cell,
    psend,
    precv,
    wsend,
    wrecv,
    above,
    below,
    wu_below,
    flipped_cols,
    ghost_rows,
    pre,
    st_rims,
    slot_source,
    slot_weight,
    split,
    payload,
    arrived,
    total,
    in_sems,
    psend_sem,
    precv_sem,
    wsend_sem,
    wrecv_sem,
    up_sems,
    down_sems,
    wub_sems,
    give_sem,
    take_sem,
):
    n_px, n_py, n_lev = sizes
    levels, tile, _ = p.shape
    last = tile - 1
    loads = [
        pltpu.make_async_copy(src, dst, in_sems.at[k])
        for k, (src, dst) in enumerate(
            (
                (p_in, p),
                (wu_in, wu),
                (owner_in, owner),
                (source_in, source),
                (weight_in, weight),
                (st_in, st),
                (we_in, we),
                (wn_in, wn),
                (cell_in, cell),
            )
        )
    ]
    for load in loads:
        load.start()
    ix, iy, iz = lax.axis_index("px"), lax.axis_index("py"), lax.axis_index("lev")
    targets = (
        {"px": lax.rem(ix + 1, n_px)},
        {"py": lax.rem(iy + 1, n_py)},
        {"px": lax.rem(ix + n_px - 1, n_px)},
        {"py": lax.rem(iy + n_py - 1, n_py)},
    )
    has_above, has_below = iz < n_lev - 1, iz > 0

    barrier = pltpu.get_barrier_semaphore()
    for target in (targets[1], targets[3]):
        pl.semaphore_signal(barrier, inc=1, device_id=target, device_id_type=MESH)

    def greet(d, carry):
        pl.semaphore_signal(barrier, inc=1, device_id={"px": lax.rem(ix + d, n_px)}, device_id_type=MESH)
        return carry

    lax.fori_loop(1, n_px, greet, 0)

    @pl.when(has_above)
    def _():
        pl.semaphore_signal(barrier, inc=1, device_id={"lev": iz + 1}, device_id_type=MESH)

    @pl.when(has_below)
    def _():
        pl.semaphore_signal(barrier, inc=1, device_id={"lev": iz - 1}, device_id_type=MESH)

    def rim_copy(send, recv, send_sem, recv_sem, t, s):
        return pltpu.make_async_remote_copy(
            src_ref=send.at[t],
            dst_ref=recv.at[t, s],
            send_sem=send_sem.at[t, s],
            recv_sem=recv_sem.at[t, s],
            device_id=targets[s],
            device_id_type=MESH,
        )

    p_copy = functools.partial(rim_copy, psend, precv, psend_sem, precv_sem)
    w_copy = functools.partial(rim_copy, wsend, wrecv, wsend_sem, wrecv_sem)

    def up_copy(t):
        return pltpu.make_async_remote_copy(
            src_ref=p.at[levels - 1],
            dst_ref=below.at[t],
            send_sem=up_sems.at[0, t],
            recv_sem=up_sems.at[1, t],
            device_id={"lev": iz + 1},
            device_id_type=MESH,
        )

    def down_copy(t):
        return pltpu.make_async_remote_copy(
            src_ref=p.at[0],
            dst_ref=above.at[t],
            send_sem=down_sems.at[0, t],
            recv_sem=down_sems.at[1, t],
            device_id={"lev": iz - 1},
            device_id_type=MESH,
        )

    def wub_copy():
        return pltpu.make_async_remote_copy(
            src_ref=wu.at[levels - 1],
            dst_ref=wu_below,
            send_sem=wub_sems.at[0],
            recv_sem=wub_sems.at[1],
            device_id={"lev": iz + 1},
            device_id_type=MESH,
        )

    row, lane = iota((tile, tile), 0), iota((tile, tile), 1)
    edge_lanes = (lane == 0) | (lane == last)
    rim_lane = iota((levels, tile), 1)
    first_lane, last_lane = rim_lane == 0, rim_lane == last

    def d_rows(f):
        return jnp.where(row == last, 0.0, pltpu.roll(f, last, 0)) - jnp.where(
            row == 0, 0.0, pltpu.roll(f, 1, 0)
        )

    def d_lanes(f):
        return jnp.where(lane == last, 0.0, pltpu.roll(f, last, 1)) - jnp.where(
            lane == 0, 0.0, pltpu.roll(f, 1, 1)
        )

    def columns(fields):
        packed = jnp.zeros((tile, tile), jnp.float32)
        for j, f in enumerate(fields):
            packed = jnp.where((lane >> 1) == j, pltpu.roll(f, 2 * j + 1, 1), packed)
        flipped_cols[...] = packed.T
        count = len(fields)
        return (
            flipped_cols[pl.ds(1, count, stride=2), :],
            flipped_cols[pl.ds(0, count, stride=2), :],
        )

    def lane_terms(south, north):
        ghost_rows[pl.ds(0, levels, stride=2), :] = north
        ghost_rows[pl.ds(1, levels, stride=2), :] = south
        turned = ghost_rows[...].T
        return [
            jnp.where(edge_lanes, pltpu.roll(turned, (tile - 2 * j - 1) % tile, 1), 0.0)
            for j in range(levels)
        ]

    codes = [edges[ix, iy, s] for s in range(4)]
    turns = [c & 3 for c in codes]
    wanted = [(s + 2 + turns[s]) & 3 for s in range(4)]
    place = iota((2 * levels, tile), 1)
    order = [jnp.where((codes[s] >> 2) == 1, last - place, place) for s in range(4)]
    low = iota((2 * levels, tile), 0) < levels

    def picked_rim(recv, t, s):
        rim = recv[t, s, 0]
        for k in range(1, 4):
            rim = jnp.where(wanted[s] == k, recv[t, s, k], rim)
        return rim

    def pressure_ghosts(t):
        ghosts = []
        for s in (0, 2):
            for k in (s, s + 1):
                p_copy(t, k).wait_recv()
            both = jnp.concatenate([picked_rim(precv, t, s), picked_rim(precv, t, s + 1)], axis=0)
            both = jnp.take_along_axis(both, jnp.where(low, order[s], order[s + 1]), axis=1)
            ghosts += [both[:levels], both[levels:]]
        return ghosts

    def wind_ghosts(t):
        ghosts = []
        for s in range(4):
            w_copy(t, s).wait_recv()
            both = jnp.take_along_axis(picked_rim(wrecv, t, s), order[s], axis=1)
            a, b = both[:levels], both[levels:]
            r = turns[s]
            if s % 2 == 0:
                ghost = jnp.where(r == 0, a, jnp.where(r == 1, -b, jnp.where(r == 2, -a, b)))
            else:
                ghost = jnp.where(r == 0, b, jnp.where(r == 1, a, jnp.where(r == 2, -b, -a)))
            ghosts.append(ghost)
        return ghosts

    def corner(first, second, end):
        if end == 0:
            return jnp.where(first_lane, first, 0.0) - jnp.where(last_lane, pltpu.roll(second, last, 1), 0.0)
        return jnp.where(first_lane, pltpu.roll(first, 1, 1), 0.0) - jnp.where(last_lane, second, 0.0)

    def give_copy(o):
        return pltpu.make_async_remote_copy(
            src_ref=payload.at[o],
            dst_ref=arrived.at[ix],
            send_sem=give_sem.at[o],
            recv_sem=take_sem.at[ix],
            device_id={"px": o},
            device_id_type=MESH,
        )

    def got(o):
        return pltpu.make_async_remote_copy(
            src_ref=payload.at[o],
            dst_ref=arrived.at[o],
            send_sem=give_sem.at[o],
            recv_sem=take_sem.at[o],
            device_id={"px": o},
            device_id_type=MESH,
        )

    loads[0].wait()
    south, north = columns([p[j] for j in range(levels)])
    psend[0, 0] = p[:, 0, :]
    psend[0, 1] = south
    psend[0, 2] = p[:, last, :]
    psend[0, 3] = north

    pl.semaphore_wait(barrier, n_px + 1 + has_above.astype(jnp.int32) + has_below.astype(jnp.int32))
    for s in range(4):
        p_copy(0, s).start()
    loads[1].wait()

    @pl.when(has_above)
    def _():
        wub_copy().start()

    @pl.when(jnp.logical_not(has_below))
    def _():
        wu_below[...] = jnp.zeros((tile, tile), jnp.float32)

    for load in loads[2:]:
        load.wait()
    ghost_rows[...] = jnp.zeros((tile, tile), jnp.float32)
    south, north = columns([st[j] for j in range(levels)])
    st_rims[0] = st[:, 0, :] * A
    st_rims[1] = south * A
    st_rims[2] = st[:, last, :] * A
    st_rims[3] = north * A
    slot_count = payload.shape[2]
    find_slots(n_px, slot_count, owner, source, weight, slot_source, slot_weight)

    def ahead(d):
        return lax.rem(ix + d + 1, n_px)

    def substep(t, carry):
        @pl.when(has_above)
        def _():
            up_copy(t).start()

        @pl.when(has_below)
        def _():
            down_copy(t).start()

        for j in range(levels):
            we[j] = we[j] - A * d_rows(p[j])
            wn[j] = wn[j] - A * d_lanes(p[j])
        south, north = columns([we[j] for j in range(levels)] + [wn[j] for j in range(levels)])
        pre[0, :levels] = we[:, 0, :]
        pre[0, levels:] = wn[:, 0, :]
        pre[1] = south
        pre[2, :levels] = we[:, last, :]
        pre[2, levels:] = wn[:, last, :]
        pre[3] = north
        for j in range(levels - 1):
            wu[j] = wu[j] - B * (p[j + 1] - p[j])

        gw, gs, ge, gn = [A * g for g in pressure_ghosts(t)]
        wsend[t, 0, :levels] = pre[0, :levels] + gw
        wsend[t, 0, levels:] = pre[0, levels:] + corner(gs, gn, 0)
        wsend[t, 1, :levels] = pre[1, :levels] + corner(gw, ge, 0)
        wsend[t, 1, levels:] = pre[1, levels:] + gs
        wsend[t, 2, :levels] = pre[2, :levels] - ge
        wsend[t, 2, levels:] = pre[2, levels:] + corner(gs, gn, last)
        wsend[t, 3, :levels] = pre[3, :levels] + corner(gw, ge, last)
        wsend[t, 3, levels:] = pre[3, levels:] - gn
        for s in range(4):
            w_copy(t, s).start()

        we[:, 0, :] = we[:, 0, :] + gw
        we[:, last, :] = we[:, last, :] - ge
        terms = lane_terms(gs, -gn)
        for j in range(levels):
            wn[j] = wn[j] + terms[j]

        @pl.when(has_above & (t == 0))
        def _():
            wub_copy().wait_send()

        @pl.when(has_above)
        def _():
            up_copy(t).wait_send()
            down_copy(t).wait_recv()
            wu[levels - 1] = wu[levels - 1] - B * (above[t] - p[levels - 1])

        @pl.when(jnp.logical_not(has_above))
        def _():
            wu[levels - 1] = jnp.zeros((tile, tile), jnp.float32)

        @pl.when(has_below & (t == 0))
        def _():
            wub_copy().wait_recv()

        @pl.when(has_below)
        def _():
            down_copy(t).wait_send()
            up_copy(t).wait_recv()
            wu_below[...] = wu_below[...] - B * (p[0] - below[t])

        for j in range(levels):
            under = wu_below[...] if j == 0 else wu[j - 1]
            p[j] = p[j] - st[j] * (A * (d_rows(we[j]) + d_lanes(wn[j])) + B * (wu[j] - under))
        south, north = columns([p[j] for j in range(levels)])
        pre[0, :levels] = p[:, 0, :]
        pre[1, :levels] = south
        pre[2, :levels] = p[:, last, :]
        pre[3, :levels] = north

        @pl.when(t == SUBSTEPS - 1)
        def _():
            for q, field in ((1, we), (2, wn), (3, wu)):
                split_field(split, field, q)
            pick(split, slot_source, slot_weight, payload, ahead(0), ahead(0), 1, 4)

        gw, gs, ge, gn = wind_ghosts(t)

        @pl.when(t < SUBSTEPS - 1)
        def _():
            psend[t + 1, 0] = pre[0, :levels] + st_rims[0] * (gw + corner(gs, gn, 0))
            psend[t + 1, 1] = pre[1, :levels] + st_rims[1] * (gs + corner(gw, ge, 0))
            psend[t + 1, 2] = pre[2, :levels] + st_rims[2] * (corner(gs, gn, last) - ge)
            psend[t + 1, 3] = pre[3, :levels] + st_rims[3] * (corner(gw, ge, last) - gn)
            for s in range(4):
                p_copy(t + 1, s).start()

        p[:, 0, :] = p[:, 0, :] + st_rims[0] * gw
        p[:, last, :] = p[:, last, :] - st_rims[2] * ge
        terms = lane_terms(st_rims[1] * gs, -(st_rims[3] * gn))
        for j in range(levels):
            p[j] = p[j] + terms[j]
        return carry

    lax.fori_loop(0, SUBSTEPS, substep, 0)

    split_field(split, p, 0)
    pick(split, slot_source, slot_weight, payload, ahead(0), ahead(0), 0, 1)
    give_copy(ahead(0)).start()

    def hand_out(d, carry):
        pick(split, slot_source, slot_weight, payload, ahead(d), ahead(d), 0, 4)
        give_copy(ahead(d)).start()
        return carry

    lax.fori_loop(1, n_px - 1, hand_out, 0)
    pick(split, slot_source, slot_weight, arrived, ix, ix, 0, 4)
    total[...] = jnp.zeros(total.shape, jnp.float32)
    land(arrived, cell, ix, total)

    def bring_in(d, carry):
        o = lax.rem(ix + n_px - d - 1, n_px)
        got(o).wait_recv()
        land(arrived, cell, o, total)
        return carry

    lax.fori_loop(0, n_px - 1, bring_in, 0)
    count, groups = 4 * levels, latlon.shape[2] // BLOCK
    for g in range(groups):
        both = total[g * count : (g + 1) * count] + total[(groups + g) * count : (groups + g + 1) * count]
        for q in range(4):
            latlon[q, :, g * BLOCK : (g + 1) * BLOCK] = both[q * levels : (q + 1) * levels]

    def drain(t, carry):
        for s in range(4):
            p_copy(t, s).wait_send()
            w_copy(t, s).wait_send()
        return carry

    lax.fori_loop(0, SUBSTEPS, drain, 0)

    def sent(d, carry):
        give_copy(ahead(d)).wait_send()
        return carry

    lax.fori_loop(0, n_px - 1, sent, 0)


def find_slots(owner_count, slot_count, owner, source, weight, slot_source, slot_weight):
    rows = owner.shape[0]
    slot_rows = slot_source.shape[0]
    names = owner[...]
    up_to = (iota((LANES, LANES), 0) <= iota((LANES, LANES), 1)).astype(jnp.bfloat16)
    ones = jnp.ones((LANES, LANES), jnp.bfloat16)
    before = (iota((rows, rows), 0) > iota((rows, rows), 1)).astype(jnp.bfloat16)

    def count(o, rank):
        named = names == o
        hot = named.astype(jnp.float32).astype(jnp.bfloat16)
        within = jnp.dot(hot, up_to, preferred_element_type=jnp.float32)
        total = jnp.dot(hot, ones, preferred_element_type=jnp.float32).astype(jnp.bfloat16)
        earlier = jnp.dot(before, total, preferred_element_type=jnp.float32)
        return jnp.where(named, within + earlier - 1.0, rank)

    rank = lax.fori_loop(0, owner_count, count, jnp.zeros(names.shape, jnp.float32))
    slot = names * slot_count + rank.astype(jnp.int32)
    slot_high, slot_low = slot >> 7, slot & (LANES - 1)
    src = source[...]
    w = weight[...]
    w1 = w.astype(jnp.bfloat16).astype(jnp.float32)
    w2 = (w - w1).astype(jnp.bfloat16).astype(jnp.float32)
    w3 = w - w1 - w2
    pieces = [(src >> 7).astype(jnp.float32), (src & (LANES - 1)).astype(jnp.float32), w1, w2, w3]
    high_place, low_place = iota((slot_rows, LANES), 0), iota((LANES, LANES), 0)
    total = jnp.zeros((len(pieces) * slot_rows, LANES), jnp.float32)
    for r in range(rows):
        here = high_place == slot_high[r : r + 1]
        left = jnp.concatenate([jnp.where(here, piece[r : r + 1], 0.0) for piece in pieces], axis=0)
        right = jnp.where(low_place == slot_low[r : r + 1], 1.0, 0.0)
        total += dot_nt(left.astype(jnp.bfloat16), right.astype(jnp.bfloat16))
    part = [total[k * slot_rows : (k + 1) * slot_rows] for k in range(len(pieces))]
    slot_source[...] = (part[0] * LANES + part[1]).astype(jnp.int32)
    slot_weight[...] = part[2] + part[3] + part[4]


def split_field(split, field, q):
    levels, tile, _ = field.shape
    half = tile // 2
    for l in range(levels):
        h, d = parts2(field[l].T)
        at = slice((q * levels + l) * half, (q * levels + l + 1) * half)
        for k, part in enumerate((h[:half], h[half:], d[:half], d[half:])):
            split[at, k * tile : (k + 1) * tile] = part


def pick(split, slot_source, slot_weight, dst, place, o, first, end):
    rows, slot_count = dst.shape[1:]
    tile = split.shape[1] // 4
    half = tile // 2
    width = min(BLOCK, slot_count)
    pieces = width // LANES
    quarter = rows // 4
    at = slice(first * quarter * half, end * quarter * half)

    def joined(ref, b):
        row = o * (slot_count // LANES) + b * pieces
        return jnp.concatenate([ref[pl.ds(row + k, 1), :] for k in range(pieces)], axis=1)

    def step(b, carry):
        src, w = joined(slot_source, b), joined(slot_weight, b)
        x, y = src >> 7, src & (tile - 1)
        line = x + jnp.where(y >= half, tile, 0)
        hot = jnp.where(iota((2 * tile, width), 0) == line, 1.0, 0.0).astype(jnp.bfloat16)
        picked = jnp.dot(
            split[at, :], jnp.concatenate([hot, hot], axis=0), preferred_element_type=jnp.float32
        )
        mask = jnp.where(iota((half, width), 0) == (y & (half - 1)), w, 0.0)
        dst[place, first * quarter : end * quarter, pl.ds(pl.multiple_of(b * width, width), width)] = jnp.sum(
            picked.reshape((end - first) * quarter, half, width) * mask[None], axis=1
        )
        return carry

    lax.fori_loop(0, slot_count // width, step, 0)


def land(arrived, cell, o, total):
    count, slot_count = arrived.shape[1:]
    groups = total.shape[0] // (2 * count)
    width = min(4 * BLOCK, slot_count)

    def step(b, carry):
        at = pl.ds(pl.multiple_of(b * width, width), width)
        c = cell[pl.ds(o, 1), at]
        values = arrived[o, :, at]
        h = values.astype(jnp.bfloat16).astype(jnp.float32)
        group = c >> 8
        spread = [jnp.where(group == g, h, 0.0) for g in range(groups)]
        spread += [jnp.where(group == g, values - h, 0.0) for g in range(groups)]
        hot = jnp.where(iota((BLOCK, width), 0) == (c & (BLOCK - 1)), 1.0, 0.0)
        total[...] += dot_nt(jnp.concatenate(spread, axis=0).astype(jnp.bfloat16), hot.astype(jnp.bfloat16))
        return carry

    lax.fori_loop(0, slot_count // width, step, 0)


def per_device(
    sizes,
    pressure,
    wind_east,
    wind_north,
    wind_up,
    stiffness,
    edge_table,
    remap_source,
    remap_weight,
    remap_owner,
    latlon_cell,
):
    levels, tile, _ = pressure.shape
    owner_count = sizes[0]
    slots = latlon_cell.shape[0]
    slot_count = slots // owner_count
    cell_count = tile * tile // 8
    count = 4 * levels
    rows = remap_source.shape[0] // LANES
    f32, i32 = jnp.float32, jnp.int32
    n = SUBSTEPS
    field = pltpu.VMEM(pressure.shape, f32)
    plane = pltpu.VMEM((tile, tile), f32)
    dma = pltpu.SemaphoreType.DMA
    in_vmem = pl.BlockSpec(memory_space=pltpu.VMEM)
    return pl.pallas_call(
        functools.partial(whole_kernel, sizes),
        out_shape=[
            jax.ShapeDtypeStruct(pressure.shape, f32),
            jax.ShapeDtypeStruct((4, levels, cell_count), f32),
        ],
        in_specs=[pl.BlockSpec(memory_space=pltpu.SMEM)] + [pl.BlockSpec(memory_space=pl.ANY)] * 9,
        out_specs=[in_vmem] * 2,
        scratch_shapes=[
            field,
            field,
            field,
            field,
            pltpu.VMEM((rows, LANES), i32),
            pltpu.VMEM((rows, LANES), i32),
            pltpu.VMEM((rows, LANES), f32),
            pltpu.VMEM((owner_count, slot_count), i32),
            pltpu.VMEM((n, 4, levels, tile), f32),
            pltpu.VMEM((n, 4, 4, levels, tile), f32),
            pltpu.VMEM((n, 4, 2 * levels, tile), f32),
            pltpu.VMEM((n, 4, 4, 2 * levels, tile), f32),
            pltpu.VMEM((n, tile, tile), f32),
            pltpu.VMEM((n, tile, tile), f32),
            plane,
            plane,
            plane,
            pltpu.VMEM((4, 2 * levels, tile), f32),
            pltpu.VMEM((4, levels, tile), f32),
            pltpu.VMEM((slots // LANES, LANES), i32),
            pltpu.VMEM((slots // LANES, LANES), f32),
            pltpu.VMEM((count * tile // 2, 4 * tile), jnp.bfloat16),
            pltpu.VMEM((owner_count, count, slot_count), f32),
            pltpu.VMEM((owner_count, count, slot_count), f32),
            pltpu.VMEM((2 * count * (cell_count // BLOCK), BLOCK), f32),
            dma((9,)),
            dma((n, 4)),
            dma((n, 4)),
            dma((n, 4)),
            dma((n, 4)),
            dma((2, n)),
            dma((2, n)),
            dma((2,)),
            dma((owner_count,)),
            dma((owner_count,)),
        ],
        compiler_params=pltpu.CompilerParams(
            collective_id=0, has_side_effects=True, vmem_limit_bytes=60 * 2**20
        ),
    )(
        edge_table,
        pressure,
        wind_east,
        wind_north,
        wind_up,
        stiffness,
        remap_owner.reshape(rows, LANES),
        remap_source.reshape(rows, LANES),
        remap_weight.reshape(rows, LANES),
        latlon_cell.reshape(owner_count, slot_count),
    )


def solution(mesh):
    field = P("lev", "px", "py")
    entries = P(("px", "py"))
    sizes = (mesh.shape["px"], mesh.shape["py"], mesh.shape["lev"])
    return jax.shard_map(
        functools.partial(per_device, sizes),
        mesh=mesh,
        in_specs=(field,) * 5 + (P(), entries, entries, P(("px", "py"), None), entries),
        out_specs=(field, P(None, "lev", ("px", "py"))),
        check_vma=False,
    )
```

```python
import functools

import jax
import jax.numpy as jnp
from jax import lax
from jax.experimental import pallas as pl
from jax.experimental.pallas import tpu as pltpu
from jax.sharding import PartitionSpec as P

SUBSTEPS = 4
A = 0.45
B = 0.3
LANES = 128
BLOCK = 256
MESH = pl.DeviceIdType.MESH


def iota(shape, dim):
    return lax.broadcasted_iota(jnp.int32, shape, dim)


def parts2(x):
    high = x.astype(jnp.bfloat16)
    return high, (x - high.astype(jnp.float32)).astype(jnp.bfloat16)


def dot_nt(a, b):
    return lax.dot_general(a, b, (((1,), (1,)), ((), ())), preferred_element_type=jnp.float32)


def whole_kernel(
    sizes,
    edges,
    p_in,
    we_in,
    wn_in,
    wu_in,
    st_in,
    owner_in,
    source_in,
    weight_in,
    cell_in,
    p,
    latlon,
    we,
    wn,
    wu,
    st,
    owner,
    source,
    weight,
    cell,
    psend,
    precv,
    wsend,
    wrecv,
    above,
    below,
    wu_below,
    flipped_cols,
    ghost_rows,
    pre,
    st_rims,
    slot_source,
    slot_weight,
    split,
    payload,
    arrived,
    total,
    in_sems,
    psend_sem,
    precv_sem,
    wsend_sem,
    wrecv_sem,
    up_sems,
    down_sems,
    wub_sems,
    give_sem,
    take_sem,
):
    n_px, n_py, n_lev = sizes
    levels, tile, _ = p.shape
    last = tile - 1
    loads = [
        pltpu.make_async_copy(src, dst, in_sems.at[k])
        for k, (src, dst) in enumerate(
            (
                (p_in, p),
                (wu_in, wu),
                (owner_in, owner),
                (source_in, source),
                (weight_in, weight),
                (st_in, st),
                (we_in, we),
                (wn_in, wn),
                (cell_in, cell),
            )
        )
    ]
    for load in loads:
        load.start()
    ix, iy, iz = lax.axis_index("px"), lax.axis_index("py"), lax.axis_index("lev")
    targets = (
        {"px": lax.rem(ix + 1, n_px)},
        {"py": lax.rem(iy + 1, n_py)},
        {"px": lax.rem(ix + n_px - 1, n_px)},
        {"py": lax.rem(iy + n_py - 1, n_py)},
    )
    has_above, has_below = iz < n_lev - 1, iz > 0

    barrier = pltpu.get_barrier_semaphore()
    for target in (targets[1], targets[3]):
        pl.semaphore_signal(barrier, inc=1, device_id=target, device_id_type=MESH)

    def greet(d, carry):
        pl.semaphore_signal(barrier, inc=1, device_id={"px": lax.rem(ix + d, n_px)}, device_id_type=MESH)
        return carry

    lax.fori_loop(1, n_px, greet, 0)

    @pl.when(has_above)
    def _():
        pl.semaphore_signal(barrier, inc=1, device_id={"lev": iz + 1}, device_id_type=MESH)

    @pl.when(has_below)
    def _():
        pl.semaphore_signal(barrier, inc=1, device_id={"lev": iz - 1}, device_id_type=MESH)

    def rim_copy(send, recv, send_sem, recv_sem, t, s):
        return pltpu.make_async_remote_copy(
            src_ref=send.at[t],
            dst_ref=recv.at[t, s],
            send_sem=send_sem.at[t, s],
            recv_sem=recv_sem.at[t, s],
            device_id=targets[s],
            device_id_type=MESH,
        )

    p_copy = functools.partial(rim_copy, psend, precv, psend_sem, precv_sem)
    w_copy = functools.partial(rim_copy, wsend, wrecv, wsend_sem, wrecv_sem)

    def up_copy(t):
        return pltpu.make_async_remote_copy(
            src_ref=p.at[levels - 1],
            dst_ref=below.at[t],
            send_sem=up_sems.at[0, t],
            recv_sem=up_sems.at[1, t],
            device_id={"lev": iz + 1},
            device_id_type=MESH,
        )

    def down_copy(t):
        return pltpu.make_async_remote_copy(
            src_ref=p.at[0],
            dst_ref=above.at[t],
            send_sem=down_sems.at[0, t],
            recv_sem=down_sems.at[1, t],
            device_id={"lev": iz - 1},
            device_id_type=MESH,
        )

    def wub_copy():
        return pltpu.make_async_remote_copy(
            src_ref=wu.at[levels - 1],
            dst_ref=wu_below,
            send_sem=wub_sems.at[0],
            recv_sem=wub_sems.at[1],
            device_id={"lev": iz + 1},
            device_id_type=MESH,
        )

    row, lane = iota((tile, tile), 0), iota((tile, tile), 1)
    edge_lanes = (lane == 0) | (lane == last)
    rim_lane = iota((levels, tile), 1)
    first_lane, last_lane = rim_lane == 0, rim_lane == last

    def d_rows(f):
        return jnp.where(row == last, 0.0, pltpu.roll(f, last, 0)) - jnp.where(
            row == 0, 0.0, pltpu.roll(f, 1, 0)
        )

    def d_lanes(f):
        return jnp.where(lane == last, 0.0, pltpu.roll(f, last, 1)) - jnp.where(
            lane == 0, 0.0, pltpu.roll(f, 1, 1)
        )

    def columns(fields):
        packed = jnp.zeros((tile, tile), jnp.float32)
        for j, f in enumerate(fields):
            packed = jnp.where((lane >> 1) == j, pltpu.roll(f, 2 * j + 1, 1), packed)
        flipped_cols[...] = packed.T
        count = len(fields)
        return (
            flipped_cols[pl.ds(1, count, stride=2), :],
            flipped_cols[pl.ds(0, count, stride=2), :],
        )

    def lane_terms(south, north):
        ghost_rows[pl.ds(0, levels, stride=2), :] = north
        ghost_rows[pl.ds(1, levels, stride=2), :] = south
        turned = ghost_rows[...].T
        return [
            jnp.where(edge_lanes, pltpu.roll(turned, (tile - 2 * j - 1) % tile, 1), 0.0)
            for j in range(levels)
        ]

    codes = [edges[ix, iy, s] for s in range(4)]
    turns = [c & 3 for c in codes]
    wanted = [(s + 2 + turns[s]) & 3 for s in range(4)]
    place = iota((2 * levels, tile), 1)
    order = [jnp.where((codes[s] >> 2) == 1, last - place, place) for s in range(4)]
    low = iota((2 * levels, tile), 0) < levels

    def picked_rim(recv, t, s):
        rim = recv[t, s, 0]
        for k in range(1, 4):
            rim = jnp.where(wanted[s] == k, recv[t, s, k], rim)
        return rim

    def pressure_ghosts(t):
        ghosts = []
        for s in (0, 2):
            for k in (s, s + 1):
                p_copy(t, k).wait_recv()
            both = jnp.concatenate([picked_rim(precv, t, s), picked_rim(precv, t, s + 1)], axis=0)
            both = jnp.take_along_axis(both, jnp.where(low, order[s], order[s + 1]), axis=1)
            ghosts += [both[:levels], both[levels:]]
        return ghosts

    def wind_ghosts(t):
        ghosts = []
        for s in range(4):
            w_copy(t, s).wait_recv()
            both = jnp.take_along_axis(picked_rim(wrecv, t, s), order[s], axis=1)
            a, b = both[:levels], both[levels:]
            r = turns[s]
            if s % 2 == 0:
                ghost = jnp.where(r == 0, a, jnp.where(r == 1, -b, jnp.where(r == 2, -a, b)))
            else:
                ghost = jnp.where(r == 0, b, jnp.where(r == 1, a, jnp.where(r == 2, -b, -a)))
            ghosts.append(ghost)
        return ghosts

    def corner(first, second, end):
        if end == 0:
            return jnp.where(first_lane, first, 0.0) - jnp.where(last_lane, pltpu.roll(second, last, 1), 0.0)
        return jnp.where(first_lane, pltpu.roll(first, 1, 1), 0.0) - jnp.where(last_lane, second, 0.0)

    def give_copy(o, k):
        part = (pl.ds(0, 3), pl.ds(3, 1))[k]
        return pltpu.make_async_remote_copy(
            src_ref=payload.at[o, part],
            dst_ref=arrived.at[ix, part],
            send_sem=give_sem.at[k, o],
            recv_sem=take_sem.at[k, ix],
            device_id={"px": o},
            device_id_type=MESH,
        )

    def got(o, k):
        part = (pl.ds(0, 3), pl.ds(3, 1))[k]
        return pltpu.make_async_remote_copy(
            src_ref=payload.at[o, part],
            dst_ref=arrived.at[o, part],
            send_sem=give_sem.at[k, o],
            recv_sem=take_sem.at[k, o],
            device_id={"px": o},
            device_id_type=MESH,
        )

    def hand_out(k):
        def give(d, carry):
            pick(split, slot_source, slot_weight, payload, ahead(d), ahead(d), 3 * k, 3 + k)
            give_copy(ahead(d), k).start()
            return carry

        lax.fori_loop(0, n_px - 1, give, 0)

    loads[0].wait()
    south, north = columns([p[j] for j in range(levels)])
    psend[0, 0] = p[:, 0, :]
    psend[0, 1] = south
    psend[0, 2] = p[:, last, :]
    psend[0, 3] = north

    pl.semaphore_wait(barrier, n_px + 1 + has_above.astype(jnp.int32) + has_below.astype(jnp.int32))
    for s in range(4):
        p_copy(0, s).start()
    loads[1].wait()

    @pl.when(has_above)
    def _():
        wub_copy().start()

    @pl.when(jnp.logical_not(has_below))
    def _():
        wu_below[...] = jnp.zeros((tile, tile), jnp.float32)

    for load in loads[2:]:
        load.wait()
    ghost_rows[...] = jnp.zeros((tile, tile), jnp.float32)
    south, north = columns([st[j] for j in range(levels)])
    st_rims[0] = st[:, 0, :] * A
    st_rims[1] = south * A
    st_rims[2] = st[:, last, :] * A
    st_rims[3] = north * A
    slot_count = payload.shape[3]
    find_slots(n_px, slot_count, owner, source, weight, slot_source, slot_weight)

    def ahead(d):
        return lax.rem(ix + d + 1, n_px)

    def substep(t, carry):
        @pl.when(has_above)
        def _():
            up_copy(t).start()

        @pl.when(has_below)
        def _():
            down_copy(t).start()

        for j in range(levels):
            we[j] = we[j] - A * d_rows(p[j])
            wn[j] = wn[j] - A * d_lanes(p[j])
        south, north = columns([we[j] for j in range(levels)] + [wn[j] for j in range(levels)])
        pre[0, :levels] = we[:, 0, :]
        pre[0, levels:] = wn[:, 0, :]
        pre[1] = south
        pre[2, :levels] = we[:, last, :]
        pre[2, levels:] = wn[:, last, :]
        pre[3] = north
        for j in range(levels - 1):
            wu[j] = wu[j] - B * (p[j + 1] - p[j])

        gw, gs, ge, gn = [A * g for g in pressure_ghosts(t)]
        wsend[t, 0, :levels] = pre[0, :levels] + gw
        wsend[t, 0, levels:] = pre[0, levels:] + corner(gs, gn, 0)
        wsend[t, 1, :levels] = pre[1, :levels] + corner(gw, ge, 0)
        wsend[t, 1, levels:] = pre[1, levels:] + gs
        wsend[t, 2, :levels] = pre[2, :levels] - ge
        wsend[t, 2, levels:] = pre[2, levels:] + corner(gs, gn, last)
        wsend[t, 3, :levels] = pre[3, :levels] + corner(gw, ge, last)
        wsend[t, 3, levels:] = pre[3, levels:] - gn
        for s in range(4):
            w_copy(t, s).start()

        we[:, 0, :] = we[:, 0, :] + gw
        we[:, last, :] = we[:, last, :] - ge
        terms = lane_terms(gs, -gn)
        for j in range(levels):
            wn[j] = wn[j] + terms[j]

        @pl.when(has_above & (t == 0))
        def _():
            wub_copy().wait_send()

        @pl.when(has_above)
        def _():
            up_copy(t).wait_send()
            down_copy(t).wait_recv()
            wu[levels - 1] = wu[levels - 1] - B * (above[t] - p[levels - 1])

        @pl.when(jnp.logical_not(has_above))
        def _():
            wu[levels - 1] = jnp.zeros((tile, tile), jnp.float32)

        @pl.when(has_below & (t == 0))
        def _():
            wub_copy().wait_recv()

        @pl.when(has_below)
        def _():
            down_copy(t).wait_send()
            up_copy(t).wait_recv()
            wu_below[...] = wu_below[...] - B * (p[0] - below[t])

        for j in range(levels):
            under = wu_below[...] if j == 0 else wu[j - 1]
            p[j] = p[j] - st[j] * (A * (d_rows(we[j]) + d_lanes(wn[j])) + B * (wu[j] - under))
        south, north = columns([p[j] for j in range(levels)])
        pre[0, :levels] = p[:, 0, :]
        pre[1, :levels] = south
        pre[2, :levels] = p[:, last, :]
        pre[3, :levels] = north

        @pl.when(t == SUBSTEPS - 1)
        def _():
            for q, field in enumerate((we, wn, wu)):
                split_field(split, field, q)
            hand_out(0)

        gw, gs, ge, gn = wind_ghosts(t)

        @pl.when(t < SUBSTEPS - 1)
        def _():
            psend[t + 1, 0] = pre[0, :levels] + st_rims[0] * (gw + corner(gs, gn, 0))
            psend[t + 1, 1] = pre[1, :levels] + st_rims[1] * (gs + corner(gw, ge, 0))
            psend[t + 1, 2] = pre[2, :levels] + st_rims[2] * (corner(gs, gn, last) - ge)
            psend[t + 1, 3] = pre[3, :levels] + st_rims[3] * (corner(gw, ge, last) - gn)
            for s in range(4):
                p_copy(t + 1, s).start()

        p[:, 0, :] = p[:, 0, :] + st_rims[0] * gw
        p[:, last, :] = p[:, last, :] - st_rims[2] * ge
        terms = lane_terms(st_rims[1] * gs, -(st_rims[3] * gn))
        for j in range(levels):
            p[j] = p[j] + terms[j]
        return carry

    lax.fori_loop(0, SUBSTEPS, substep, 0)

    split_field(split, p, 3)
    hand_out(1)
    pick(split, slot_source, slot_weight, arrived, ix, ix, 0, 4)
    total[...] = jnp.zeros(total.shape, jnp.float32)
    land(arrived, cell, ix, total)

    def bring_in(d, carry):
        o = lax.rem(ix + n_px - d - 1, n_px)
        got(o, 0).wait_recv()
        got(o, 1).wait_recv()
        land(arrived, cell, o, total)
        return carry

    lax.fori_loop(0, n_px - 1, bring_in, 0)
    count, groups = 4 * levels, latlon.shape[2] // BLOCK
    for g in range(groups):
        both = total[g * count : (g + 1) * count] + total[(groups + g) * count : (groups + g + 1) * count]
        for q in range(4):
            latlon[(q + 1) % 4, :, g * BLOCK : (g + 1) * BLOCK] = both[q * levels : (q + 1) * levels]

    def drain(t, carry):
        for s in range(4):
            p_copy(t, s).wait_send()
            w_copy(t, s).wait_send()
        return carry

    lax.fori_loop(0, SUBSTEPS, drain, 0)

    def sent(d, carry):
        give_copy(ahead(d), 0).wait_send()
        give_copy(ahead(d), 1).wait_send()
        return carry

    lax.fori_loop(0, n_px - 1, sent, 0)


def find_slots(owner_count, slot_count, owner, source, weight, slot_source, slot_weight):
    rows = owner.shape[0]
    slot_rows = slot_source.shape[0]
    names = owner[...]
    up_to = (iota((LANES, LANES), 0) <= iota((LANES, LANES), 1)).astype(jnp.bfloat16)
    ones = jnp.ones((LANES, LANES), jnp.bfloat16)
    before = (iota((rows, rows), 0) > iota((rows, rows), 1)).astype(jnp.bfloat16)

    def count(o, rank):
        named = names == o
        hot = named.astype(jnp.float32).astype(jnp.bfloat16)
        within = jnp.dot(hot, up_to, preferred_element_type=jnp.float32)
        total = jnp.dot(hot, ones, preferred_element_type=jnp.float32).astype(jnp.bfloat16)
        earlier = jnp.dot(before, total, preferred_element_type=jnp.float32)
        return jnp.where(named, within + earlier - 1.0, rank)

    rank = lax.fori_loop(0, owner_count, count, jnp.zeros(names.shape, jnp.float32))
    slot = names * slot_count + rank.astype(jnp.int32)
    slot_high, slot_low = slot >> 7, slot & (LANES - 1)
    src = source[...]
    w = weight[...]
    w1 = w.astype(jnp.bfloat16).astype(jnp.float32)
    w2 = (w - w1).astype(jnp.bfloat16).astype(jnp.float32)
    w3 = w - w1 - w2
    pieces = [(src >> 7).astype(jnp.float32), (src & (LANES - 1)).astype(jnp.float32), w1, w2, w3]
    high_place, low_place = iota((slot_rows, LANES), 0), iota((LANES, LANES), 0)
    total = jnp.zeros((len(pieces) * slot_rows, LANES), jnp.float32)
    for r in range(rows):
        here = high_place == slot_high[r : r + 1]
        left = jnp.concatenate([jnp.where(here, piece[r : r + 1], 0.0) for piece in pieces], axis=0)
        right = jnp.where(low_place == slot_low[r : r + 1], 1.0, 0.0)
        total += dot_nt(left.astype(jnp.bfloat16), right.astype(jnp.bfloat16))
    part = [total[k * slot_rows : (k + 1) * slot_rows] for k in range(len(pieces))]
    slot_source[...] = (part[0] * LANES + part[1]).astype(jnp.int32)
    slot_weight[...] = part[2] + part[3] + part[4]


def split_field(split, field, q):
    levels, tile, _ = field.shape
    half = tile // 2
    for l in range(levels):
        h, d = parts2(field[l].T)
        at = slice((q * levels + l) * half, (q * levels + l + 1) * half)
        for k, part in enumerate((h[:half], h[half:], d[:half], d[half:])):
            split[at, k * tile : (k + 1) * tile] = part


def pick(split, slot_source, slot_weight, dst, place, o, first, end):
    _, _, quarter, slot_count = dst.shape
    tile = split.shape[1] // 4
    half = tile // 2
    width = min(BLOCK, slot_count)
    pieces = width // LANES
    at = slice(first * quarter * half, end * quarter * half)

    def joined(ref, b):
        row = o * (slot_count // LANES) + b * pieces
        return jnp.concatenate([ref[pl.ds(row + k, 1), :] for k in range(pieces)], axis=1)

    def step(b, carry):
        src, w = joined(slot_source, b), joined(slot_weight, b)
        x, y = src >> 7, src & (tile - 1)
        line = x + jnp.where(y >= half, tile, 0)
        hot = jnp.where(iota((2 * tile, width), 0) == line, 1.0, 0.0).astype(jnp.bfloat16)
        picked = jnp.dot(
            split[at, :], jnp.concatenate([hot, hot], axis=0), preferred_element_type=jnp.float32
        )
        mask = jnp.where(iota((half, width), 0) == (y & (half - 1)), w, 0.0)
        taken = jnp.sum(picked.reshape((end - first) * quarter, half, width) * mask[None], axis=1)
        for q in range(first, end):
            dst[place, q, :, pl.ds(pl.multiple_of(b * width, width), width)] = taken[
                (q - first) * quarter : (q - first + 1) * quarter
            ]
        return carry

    lax.fori_loop(0, slot_count // width, step, 0)


def land(arrived, cell, o, total):
    _, parts, levels, slot_count = arrived.shape
    count = parts * levels
    groups = total.shape[0] // (2 * count)
    width = min(4 * BLOCK, slot_count)

    def step(b, carry):
        at = pl.ds(pl.multiple_of(b * width, width), width)
        row = o * (slot_count // LANES) + b * (width // LANES)
        c = jnp.concatenate([cell[pl.ds(row + k, 1), :] for k in range(width // LANES)], axis=1)
        values = jnp.concatenate([arrived[o, q, :, at] for q in range(parts)], axis=0)
        h = values.astype(jnp.bfloat16).astype(jnp.float32)
        group = c >> 8
        spread = [jnp.where(group == g, h, 0.0) for g in range(groups)]
        spread += [jnp.where(group == g, values - h, 0.0) for g in range(groups)]
        hot = jnp.where(iota((BLOCK, width), 0) == (c & (BLOCK - 1)), 1.0, 0.0)
        total[...] += dot_nt(jnp.concatenate(spread, axis=0).astype(jnp.bfloat16), hot.astype(jnp.bfloat16))
        return carry

    lax.fori_loop(0, slot_count // width, step, 0)


def per_device(
    sizes,
    pressure,
    wind_east,
    wind_north,
    wind_up,
    stiffness,
    edge_table,
    remap_source,
    remap_weight,
    remap_owner,
    latlon_cell,
):
    levels, tile, _ = pressure.shape
    owner_count = sizes[0]
    slots = latlon_cell.shape[0]
    slot_count = slots // owner_count
    cell_count = tile * tile // 8
    count = 4 * levels
    rows = remap_source.shape[0] // LANES
    f32, i32 = jnp.float32, jnp.int32
    n = SUBSTEPS
    field = pltpu.VMEM(pressure.shape, f32)
    plane = pltpu.VMEM((tile, tile), f32)
    dma = pltpu.SemaphoreType.DMA
    in_vmem = pl.BlockSpec(memory_space=pltpu.VMEM)
    return pl.pallas_call(
        functools.partial(whole_kernel, sizes),
        out_shape=[
            jax.ShapeDtypeStruct(pressure.shape, f32),
            jax.ShapeDtypeStruct((4, levels, cell_count), f32),
        ],
        in_specs=[pl.BlockSpec(memory_space=pltpu.SMEM)] + [pl.BlockSpec(memory_space=pl.ANY)] * 9,
        out_specs=[in_vmem] * 2,
        scratch_shapes=[
            field,
            field,
            field,
            field,
            pltpu.VMEM((rows, LANES), i32),
            pltpu.VMEM((rows, LANES), i32),
            pltpu.VMEM((rows, LANES), f32),
            pltpu.VMEM((slots // LANES, LANES), i32),
            pltpu.VMEM((n, 4, levels, tile), f32),
            pltpu.VMEM((n, 4, 4, levels, tile), f32),
            pltpu.VMEM((n, 4, 2 * levels, tile), f32),
            pltpu.VMEM((n, 4, 4, 2 * levels, tile), f32),
            pltpu.VMEM((n, tile, tile), f32),
            pltpu.VMEM((n, tile, tile), f32),
            plane,
            plane,
            plane,
            pltpu.VMEM((4, 2 * levels, tile), f32),
            pltpu.VMEM((4, levels, tile), f32),
            pltpu.VMEM((slots // LANES, LANES), i32),
            pltpu.VMEM((slots // LANES, LANES), f32),
            pltpu.VMEM((count * tile // 2, 4 * tile), jnp.bfloat16),
            pltpu.VMEM((owner_count, 4, levels, slot_count), f32),
            pltpu.VMEM((owner_count, 4, levels, slot_count), f32),
            pltpu.VMEM((2 * count * (cell_count // BLOCK), BLOCK), f32),
            dma((9,)),
            dma((n, 4)),
            dma((n, 4)),
            dma((n, 4)),
            dma((n, 4)),
            dma((2, n)),
            dma((2, n)),
            dma((2,)),
            dma((2, owner_count)),
            dma((2, owner_count)),
        ],
        compiler_params=pltpu.CompilerParams(
            collective_id=0, has_side_effects=True, vmem_limit_bytes=60 * 2**20
        ),
    )(
        edge_table,
        pressure,
        wind_east,
        wind_north,
        wind_up,
        stiffness,
        remap_owner.reshape(rows, LANES),
        remap_source.reshape(rows, LANES),
        remap_weight.reshape(rows, LANES),
        latlon_cell.reshape(slots // LANES, LANES),
    )


def solution(mesh):
    field = P("lev", "px", "py")
    entries = P(("px", "py"))
    sizes = (mesh.shape["px"], mesh.shape["py"], mesh.shape["lev"])
    return jax.shard_map(
        functools.partial(per_device, sizes),
        mesh=mesh,
        in_specs=(field,) * 5 + (P(), entries, entries, P(("px", "py"), None), entries),
        out_specs=(field, P(None, "lev", ("px", "py"))),
        check_vma=False,
    )
```

```python
import functools

import jax
import jax.numpy as jnp
from jax import lax
from jax.experimental import pallas as pl
from jax.experimental.pallas import tpu as pltpu
from jax.sharding import PartitionSpec as P

SUBSTEPS = 4
A = 0.45
B = 0.3
LANES = 128
BLOCK = 256
MESH = pl.DeviceIdType.MESH


def iota(shape, dim):
    return lax.broadcasted_iota(jnp.int32, shape, dim)


def parts2(x):
    high = x.astype(jnp.bfloat16)
    return high, (x - high.astype(jnp.float32)).astype(jnp.bfloat16)


def dot_nt(a, b):
    return lax.dot_general(a, b, (((1,), (1,)), ((), ())), preferred_element_type=jnp.float32)


def whole_kernel(
    sizes,
    edges,
    p_in,
    we_in,
    wn_in,
    wu_in,
    st_in,
    owner_in,
    source_in,
    weight_in,
    cell_in,
    p,
    latlon,
    we,
    wn,
    wu,
    st,
    owner,
    source,
    weight,
    cell,
    psend,
    precv,
    wsend,
    wrecv,
    above,
    below,
    wu_below,
    flipped_cols,
    ghost_rows,
    pre,
    st_rims,
    slot_source,
    slot_weight,
    split,
    payload,
    arrived,
    total,
    in_sems,
    psend_sem,
    precv_sem,
    wsend_sem,
    wrecv_sem,
    up_sems,
    down_sems,
    wub_sems,
    give_sem,
    take_sem,
):
    n_px, n_py, n_lev = sizes
    levels, tile, _ = p.shape
    last = tile - 1
    loads = [
        pltpu.make_async_copy(src, dst, in_sems.at[k])
        for k, (src, dst) in enumerate(
            (
                (p_in, p),
                (wu_in, wu),
                (owner_in, owner),
                (source_in, source),
                (weight_in, weight),
                (st_in, st),
                (we_in, we),
                (wn_in, wn),
                (cell_in, cell),
            )
        )
    ]
    for load in loads:
        load.start()
    ix, iy, iz = lax.axis_index("px"), lax.axis_index("py"), lax.axis_index("lev")
    targets = (
        {"px": lax.rem(ix + 1, n_px)},
        {"py": lax.rem(iy + 1, n_py)},
        {"px": lax.rem(ix + n_px - 1, n_px)},
        {"py": lax.rem(iy + n_py - 1, n_py)},
    )
    has_above, has_below = iz < n_lev - 1, iz > 0

    barrier = pltpu.get_barrier_semaphore()
    for target in (targets[1], targets[3]):
        pl.semaphore_signal(barrier, inc=1, device_id=target, device_id_type=MESH)

    def greet(d, carry):
        pl.semaphore_signal(barrier, inc=1, device_id={"px": lax.rem(ix + d, n_px)}, device_id_type=MESH)
        return carry

    lax.fori_loop(1, n_px, greet, 0)

    @pl.when(has_above)
    def _():
        pl.semaphore_signal(barrier, inc=1, device_id={"lev": iz + 1}, device_id_type=MESH)

    @pl.when(has_below)
    def _():
        pl.semaphore_signal(barrier, inc=1, device_id={"lev": iz - 1}, device_id_type=MESH)

    def rim_copy(send, recv, send_sem, recv_sem, t, s):
        return pltpu.make_async_remote_copy(
            src_ref=send.at[t],
            dst_ref=recv.at[t, s],
            send_sem=send_sem.at[t, s],
            recv_sem=recv_sem.at[t, s],
            device_id=targets[s],
            device_id_type=MESH,
        )

    p_copy = functools.partial(rim_copy, psend, precv, psend_sem, precv_sem)
    w_copy = functools.partial(rim_copy, wsend, wrecv, wsend_sem, wrecv_sem)

    def up_copy(t):
        return pltpu.make_async_remote_copy(
            src_ref=p.at[levels - 1],
            dst_ref=below.at[t],
            send_sem=up_sems.at[0, t],
            recv_sem=up_sems.at[1, t],
            device_id={"lev": iz + 1},
            device_id_type=MESH,
        )

    def down_copy(t):
        return pltpu.make_async_remote_copy(
            src_ref=p.at[0],
            dst_ref=above.at[t],
            send_sem=down_sems.at[0, t],
            recv_sem=down_sems.at[1, t],
            device_id={"lev": iz - 1},
            device_id_type=MESH,
        )

    def wub_copy():
        return pltpu.make_async_remote_copy(
            src_ref=wu.at[levels - 1],
            dst_ref=wu_below,
            send_sem=wub_sems.at[0],
            recv_sem=wub_sems.at[1],
            device_id={"lev": iz + 1},
            device_id_type=MESH,
        )

    row, lane = iota((tile, tile), 0), iota((tile, tile), 1)
    edge_lanes = (lane == 0) | (lane == last)
    rim_lane = iota((levels, tile), 1)
    first_lane, last_lane = rim_lane == 0, rim_lane == last

    def d_rows(f):
        return jnp.where(row == last, 0.0, pltpu.roll(f, last, 0)) - jnp.where(
            row == 0, 0.0, pltpu.roll(f, 1, 0)
        )

    def d_lanes(f):
        return jnp.where(lane == last, 0.0, pltpu.roll(f, last, 1)) - jnp.where(
            lane == 0, 0.0, pltpu.roll(f, 1, 1)
        )

    def columns(fields):
        packed = jnp.zeros((tile, tile), jnp.float32)
        for j, f in enumerate(fields):
            packed = jnp.where((lane >> 1) == j, pltpu.roll(f, 2 * j + 1, 1), packed)
        flipped_cols[...] = packed.T
        count = len(fields)
        return (
            flipped_cols[pl.ds(1, count, stride=2), :],
            flipped_cols[pl.ds(0, count, stride=2), :],
        )

    def lane_terms(south, north):
        ghost_rows[pl.ds(0, levels, stride=2), :] = north
        ghost_rows[pl.ds(1, levels, stride=2), :] = south
        turned = ghost_rows[...].T
        return [
            jnp.where(edge_lanes, pltpu.roll(turned, (tile - 2 * j - 1) % tile, 1), 0.0)
            for j in range(levels)
        ]

    codes = [edges[ix, iy, s] for s in range(4)]
    turns = [c & 3 for c in codes]
    wanted = [(s + 2 + turns[s]) & 3 for s in range(4)]
    place = iota((2 * levels, tile), 1)
    order = [jnp.where((codes[s] >> 2) == 1, last - place, place) for s in range(4)]
    low = iota((2 * levels, tile), 0) < levels

    def picked_rim(recv, t, s):
        rim = recv[t, s, 0]
        for k in range(1, 4):
            rim = jnp.where(wanted[s] == k, recv[t, s, k], rim)
        return rim

    def pressure_ghosts(t):
        ghosts = []
        for s in (0, 2):
            for k in (s, s + 1):
                p_copy(t, k).wait_recv()
            both = jnp.concatenate([picked_rim(precv, t, s), picked_rim(precv, t, s + 1)], axis=0)
            both = jnp.take_along_axis(both, jnp.where(low, order[s], order[s + 1]), axis=1)
            ghosts += [both[:levels], both[levels:]]
        return ghosts

    def wind_ghosts(t):
        ghosts = []
        for s in range(4):
            w_copy(t, s).wait_recv()
            both = jnp.take_along_axis(picked_rim(wrecv, t, s), order[s], axis=1)
            a, b = both[:levels], both[levels:]
            r = turns[s]
            if s % 2 == 0:
                ghost = jnp.where(r == 0, a, jnp.where(r == 1, -b, jnp.where(r == 2, -a, b)))
            else:
                ghost = jnp.where(r == 0, b, jnp.where(r == 1, a, jnp.where(r == 2, -b, -a)))
            ghosts.append(ghost)
        return ghosts

    def corner(first, second, end):
        if end == 0:
            return jnp.where(first_lane, first, 0.0) - jnp.where(last_lane, pltpu.roll(second, last, 1), 0.0)
        return jnp.where(first_lane, pltpu.roll(first, 1, 1), 0.0) - jnp.where(last_lane, second, 0.0)

    def give_copy(o):
        return pltpu.make_async_remote_copy(
            src_ref=payload.at[o],
            dst_ref=arrived.at[ix],
            send_sem=give_sem.at[o],
            recv_sem=take_sem.at[ix],
            device_id={"px": o},
            device_id_type=MESH,
        )

    def got(o):
        return pltpu.make_async_remote_copy(
            src_ref=payload.at[o],
            dst_ref=arrived.at[o],
            send_sem=give_sem.at[o],
            recv_sem=take_sem.at[o],
            device_id={"px": o},
            device_id_type=MESH,
        )

    loads[0].wait()
    south, north = columns([p[j] for j in range(levels)])
    psend[0, 0] = p[:, 0, :]
    psend[0, 1] = south
    psend[0, 2] = p[:, last, :]
    psend[0, 3] = north

    pl.semaphore_wait(barrier, n_px + 1 + has_above.astype(jnp.int32) + has_below.astype(jnp.int32))
    for s in range(4):
        p_copy(0, s).start()
    loads[1].wait()

    @pl.when(has_above)
    def _():
        wub_copy().start()

    @pl.when(jnp.logical_not(has_below))
    def _():
        wu_below[...] = jnp.zeros((tile, tile), jnp.float32)

    for load in loads[2:]:
        load.wait()
    ghost_rows[...] = jnp.zeros((tile, tile), jnp.float32)
    south, north = columns([st[j] for j in range(levels)])
    st_rims[0] = st[:, 0, :] * A
    st_rims[1] = south * A
    st_rims[2] = st[:, last, :] * A
    st_rims[3] = north * A
    slot_count = payload.shape[2]
    find_slots(n_px, slot_count, owner, source, weight, slot_source, slot_weight)

    def ahead(d):
        return lax.rem(ix + d + 1, n_px)

    def substep(t, carry):
        @pl.when(has_above)
        def _():
            up_copy(t).start()

        @pl.when(has_below)
        def _():
            down_copy(t).start()

        for j in range(levels):
            we[j] = we[j] - A * d_rows(p[j])
            wn[j] = wn[j] - A * d_lanes(p[j])
        south, north = columns([we[j] for j in range(levels)] + [wn[j] for j in range(levels)])
        pre[0, :levels] = we[:, 0, :]
        pre[0, levels:] = wn[:, 0, :]
        pre[1] = south
        pre[2, :levels] = we[:, last, :]
        pre[2, levels:] = wn[:, last, :]
        pre[3] = north
        for j in range(levels - 1):
            wu[j] = wu[j] - B * (p[j + 1] - p[j])

        gw, gs, ge, gn = [A * g for g in pressure_ghosts(t)]
        wsend[t, 0, :levels] = pre[0, :levels] + gw
        wsend[t, 0, levels:] = pre[0, levels:] + corner(gs, gn, 0)
        wsend[t, 1, :levels] = pre[1, :levels] + corner(gw, ge, 0)
        wsend[t, 1, levels:] = pre[1, levels:] + gs
        wsend[t, 2, :levels] = pre[2, :levels] - ge
        wsend[t, 2, levels:] = pre[2, levels:] + corner(gs, gn, last)
        wsend[t, 3, :levels] = pre[3, :levels] + corner(gw, ge, last)
        wsend[t, 3, levels:] = pre[3, levels:] - gn
        for s in range(4):
            w_copy(t, s).start()

        we[:, 0, :] = we[:, 0, :] + gw
        we[:, last, :] = we[:, last, :] - ge
        terms = lane_terms(gs, -gn)
        for j in range(levels):
            wn[j] = wn[j] + terms[j]

        @pl.when(has_above & (t == 0))
        def _():
            wub_copy().wait_send()

        @pl.when(has_above)
        def _():
            up_copy(t).wait_send()
            down_copy(t).wait_recv()
            wu[levels - 1] = wu[levels - 1] - B * (above[t] - p[levels - 1])

        @pl.when(jnp.logical_not(has_above))
        def _():
            wu[levels - 1] = jnp.zeros((tile, tile), jnp.float32)

        @pl.when(has_below & (t == 0))
        def _():
            wub_copy().wait_recv()

        @pl.when(has_below)
        def _():
            down_copy(t).wait_send()
            up_copy(t).wait_recv()
            wu_below[...] = wu_below[...] - B * (p[0] - below[t])

        for j in range(levels):
            under = wu_below[...] if j == 0 else wu[j - 1]
            p[j] = p[j] - st[j] * (A * (d_rows(we[j]) + d_lanes(wn[j])) + B * (wu[j] - under))
        south, north = columns([p[j] for j in range(levels)])
        pre[0, :levels] = p[:, 0, :]
        pre[1, :levels] = south
        pre[2, :levels] = p[:, last, :]
        pre[3, :levels] = north

        @pl.when(t == SUBSTEPS - 1)
        def _():
            for q, field in ((1, we), (2, wn), (3, wu)):
                split_field(split, field, q)
            pick(split, slot_source, slot_weight, payload, ahead(0), ahead(0), 1, 4)

        gw, gs, ge, gn = wind_ghosts(t)

        @pl.when(t < SUBSTEPS - 1)
        def _():
            psend[t + 1, 0] = pre[0, :levels] + st_rims[0] * (gw + corner(gs, gn, 0))
            psend[t + 1, 1] = pre[1, :levels] + st_rims[1] * (gs + corner(gw, ge, 0))
            psend[t + 1, 2] = pre[2, :levels] + st_rims[2] * (corner(gs, gn, last) - ge)
            psend[t + 1, 3] = pre[3, :levels] + st_rims[3] * (corner(gw, ge, last) - gn)
            for s in range(4):
                p_copy(t + 1, s).start()

        p[:, 0, :] = p[:, 0, :] + st_rims[0] * gw
        p[:, last, :] = p[:, last, :] - st_rims[2] * ge
        terms = lane_terms(st_rims[1] * gs, -(st_rims[3] * gn))
        for j in range(levels):
            p[j] = p[j] + terms[j]
        return carry

    lax.fori_loop(0, SUBSTEPS, substep, 0)

    split_field(split, p, 0)
    pick(split, slot_source, slot_weight, payload, ahead(0), ahead(0), 0, 1)
    give_copy(ahead(0)).start()

    def hand_out(d, carry):
        pick(split, slot_source, slot_weight, payload, ahead(d), ahead(d), 0, 4)
        give_copy(ahead(d)).start()
        return carry

    lax.fori_loop(1, n_px - 1, hand_out, 0)
    pick(split, slot_source, slot_weight, arrived, ix, ix, 0, 4)
    total[...] = jnp.zeros(total.shape, jnp.float32)
    land(arrived, cell, ix, total)

    def bring_in(d, carry):
        o = lax.rem(ix + n_px - d - 1, n_px)
        got(o).wait_recv()
        land(arrived, cell, o, total)
        return carry

    lax.fori_loop(0, n_px - 1, bring_in, 0)
    count, groups = 4 * levels, latlon.shape[2] // BLOCK
    for g in range(groups):
        both = total[g * count : (g + 1) * count] + total[(groups + g) * count : (groups + g + 1) * count]
        for q in range(4):
            latlon[q, :, g * BLOCK : (g + 1) * BLOCK] = both[q * levels : (q + 1) * levels]

    def drain(t, carry):
        for s in range(4):
            p_copy(t, s).wait_send()
            w_copy(t, s).wait_send()
        return carry

    lax.fori_loop(0, SUBSTEPS, drain, 0)

    def sent(d, carry):
        give_copy(ahead(d)).wait_send()
        return carry

    lax.fori_loop(0, n_px - 1, sent, 0)


def find_slots(owner_count, slot_count, owner, source, weight, slot_source, slot_weight):
    rows = owner.shape[0]
    slot_rows = slot_source.shape[0]
    names = owner[...]
    up_to = (iota((LANES, LANES), 0) <= iota((LANES, LANES), 1)).astype(jnp.bfloat16)
    ones = jnp.ones((LANES, LANES), jnp.bfloat16)
    before = (iota((rows, rows), 0) > iota((rows, rows), 1)).astype(jnp.bfloat16)

    def count(o, rank):
        named = names == o
        hot = named.astype(jnp.float32).astype(jnp.bfloat16)
        within = jnp.dot(hot, up_to, preferred_element_type=jnp.float32)
        total = jnp.dot(hot, ones, preferred_element_type=jnp.float32).astype(jnp.bfloat16)
        earlier = jnp.dot(before, total, preferred_element_type=jnp.float32)
        return jnp.where(named, within + earlier - 1.0, rank)

    rank = lax.fori_loop(0, owner_count, count, jnp.zeros(names.shape, jnp.float32))
    slot = names * slot_count + rank.astype(jnp.int32)
    slot_high, slot_low = slot >> 7, slot & (LANES - 1)
    src = source[...]
    w = weight[...]
    w1 = w.astype(jnp.bfloat16).astype(jnp.float32)
    w2 = (w - w1).astype(jnp.bfloat16).astype(jnp.float32)
    w3 = w - w1 - w2
    pieces = [(src >> 7).astype(jnp.float32), (src & (LANES - 1)).astype(jnp.float32), w1, w2, w3]
    high_place, low_place = iota((slot_rows, LANES), 0), iota((LANES, LANES), 0)
    total = jnp.zeros((len(pieces) * slot_rows, LANES), jnp.float32)
    for r in range(rows):
        here = high_place == slot_high[r : r + 1]
        left = jnp.concatenate([jnp.where(here, piece[r : r + 1], 0.0) for piece in pieces], axis=0)
        right = jnp.where(low_place == slot_low[r : r + 1], 1.0, 0.0)
        total += dot_nt(left.astype(jnp.bfloat16), right.astype(jnp.bfloat16))
    part = [total[k * slot_rows : (k + 1) * slot_rows] for k in range(len(pieces))]
    slot_source[...] = (part[0] * LANES + part[1]).astype(jnp.int32)
    slot_weight[...] = part[2] + part[3] + part[4]


def split_field(split, field, q):
    levels, tile, _ = field.shape
    half = tile // 2
    for l in range(levels):
        h, d = parts2(field[l].T)
        at = slice((q * levels + l) * half, (q * levels + l + 1) * half)
        for k, part in enumerate((h[:half], h[half:], d[:half], d[half:])):
            split[at, k * tile : (k + 1) * tile] = part


def pick(split, slot_source, slot_weight, dst, place, o, first, end):
    rows, slot_count = dst.shape[1:]
    tile = split.shape[1] // 4
    half = tile // 2
    width = min(BLOCK, slot_count)
    pieces = width // LANES
    quarter = rows // 4
    at = slice(first * quarter * half, end * quarter * half)

    def joined(ref, b):
        row = o * (slot_count // LANES) + b * pieces
        return jnp.concatenate([ref[pl.ds(row + k, 1), :] for k in range(pieces)], axis=1)

    def step(b, carry):
        src, w = joined(slot_source, b), joined(slot_weight, b)
        x, y = src >> 7, src & (tile - 1)
        line = x + jnp.where(y >= half, tile, 0)
        hot = jnp.where(iota((2 * tile, width), 0) == line, 1.0, 0.0).astype(jnp.bfloat16)
        picked = jnp.dot(
            split[at, :], jnp.concatenate([hot, hot], axis=0), preferred_element_type=jnp.float32
        )
        mask = jnp.where(iota((half, width), 0) == (y & (half - 1)), w, 0.0)
        dst[place, first * quarter : end * quarter, pl.ds(pl.multiple_of(b * width, width), width)] = jnp.sum(
            picked.reshape((end - first) * quarter, half, width) * mask[None], axis=1
        )
        return carry

    lax.fori_loop(0, slot_count // width, step, 0)


def land(arrived, cell, o, total):
    count, slot_count = arrived.shape[1:]
    groups = total.shape[0] // (2 * count)
    width = min(4 * BLOCK, slot_count)

    def step(b, carry):
        at = pl.ds(pl.multiple_of(b * width, width), width)
        row = o * (slot_count // LANES) + b * (width // LANES)
        c = jnp.concatenate([cell[pl.ds(row + k, 1), :] for k in range(width // LANES)], axis=1)
        values = arrived[o, :, at]
        h = values.astype(jnp.bfloat16).astype(jnp.float32)
        group = c >> 8
        spread = [jnp.where(group == g, h, 0.0) for g in range(groups)]
        spread += [jnp.where(group == g, values - h, 0.0) for g in range(groups)]
        hot = jnp.where(iota((BLOCK, width), 0) == (c & (BLOCK - 1)), 1.0, 0.0)
        total[...] += dot_nt(jnp.concatenate(spread, axis=0).astype(jnp.bfloat16), hot.astype(jnp.bfloat16))
        return carry

    lax.fori_loop(0, slot_count // width, step, 0)


def per_device(
    sizes,
    pressure,
    wind_east,
    wind_north,
    wind_up,
    stiffness,
    edge_table,
    remap_source,
    remap_weight,
    remap_owner,
    latlon_cell,
):
    levels, tile, _ = pressure.shape
    owner_count = sizes[0]
    slots = latlon_cell.shape[0]
    slot_count = slots // owner_count
    cell_count = tile * tile // 8
    count = 4 * levels
    rows = remap_source.shape[0] // LANES
    f32, i32 = jnp.float32, jnp.int32
    n = SUBSTEPS
    field = pltpu.VMEM(pressure.shape, f32)
    plane = pltpu.VMEM((tile, tile), f32)
    dma = pltpu.SemaphoreType.DMA
    in_vmem = pl.BlockSpec(memory_space=pltpu.VMEM)
    return pl.pallas_call(
        functools.partial(whole_kernel, sizes),
        out_shape=[
            jax.ShapeDtypeStruct(pressure.shape, f32),
            jax.ShapeDtypeStruct((4, levels, cell_count), f32),
        ],
        in_specs=[pl.BlockSpec(memory_space=pltpu.SMEM)] + [pl.BlockSpec(memory_space=pl.ANY)] * 9,
        out_specs=[in_vmem] * 2,
        scratch_shapes=[
            field,
            field,
            field,
            field,
            pltpu.VMEM((rows, LANES), i32),
            pltpu.VMEM((rows, LANES), i32),
            pltpu.VMEM((rows, LANES), f32),
            pltpu.VMEM((slots // LANES, LANES), i32),
            pltpu.VMEM((n, 4, levels, tile), f32),
            pltpu.VMEM((n, 4, 4, levels, tile), f32),
            pltpu.VMEM((n, 4, 2 * levels, tile), f32),
            pltpu.VMEM((n, 4, 4, 2 * levels, tile), f32),
            pltpu.VMEM((n, tile, tile), f32),
            pltpu.VMEM((n, tile, tile), f32),
            plane,
            plane,
            plane,
            pltpu.VMEM((4, 2 * levels, tile), f32),
            pltpu.VMEM((4, levels, tile), f32),
            pltpu.VMEM((slots // LANES, LANES), i32),
            pltpu.VMEM((slots // LANES, LANES), f32),
            pltpu.VMEM((count * tile // 2, 4 * tile), jnp.bfloat16),
            pltpu.VMEM((owner_count, count, slot_count), f32),
            pltpu.VMEM((owner_count, count, slot_count), f32),
            pltpu.VMEM((2 * count * (cell_count // BLOCK), BLOCK), f32),
            dma((9,)),
            dma((n, 4)),
            dma((n, 4)),
            dma((n, 4)),
            dma((n, 4)),
            dma((2, n)),
            dma((2, n)),
            dma((2,)),
            dma((owner_count,)),
            dma((owner_count,)),
        ],
        compiler_params=pltpu.CompilerParams(
            collective_id=0, has_side_effects=True, vmem_limit_bytes=60 * 2**20
        ),
    )(
        edge_table,
        pressure,
        wind_east,
        wind_north,
        wind_up,
        stiffness,
        remap_owner.reshape(rows, LANES),
        remap_source.reshape(rows, LANES),
        remap_weight.reshape(rows, LANES),
        latlon_cell.reshape(slots // LANES, LANES),
    )


def solution(mesh):
    field = P("lev", "px", "py")
    entries = P(("px", "py"))
    sizes = (mesh.shape["px"], mesh.shape["py"], mesh.shape["lev"])
    return jax.shard_map(
        functools.partial(per_device, sizes),
        mesh=mesh,
        in_specs=(field,) * 5 + (P(), entries, entries, P(("px", "py"), None), entries),
        out_specs=(field, P(None, "lev", ("px", "py"))),
        check_vma=False,
    )
```
